128 devices in a mesh: tm: 4 (over y_lo, core), space: 32 (over x, y_hi, z).
Axes of the slice: x: 4, y: 4 (y_hi: 2, y_lo: 2; y = y_hi * 2 + y_lo), z: 4, core: 2. Of those that a mesh axis runs over, the one named last changes fastest.
Arguments:
- features: bfloat16 [8, 128, 128, 128], P('tm', 'space'), may hold values from -6 to 6
- weight_a: bfloat16 [3, 3, 3, 128, 256], replicated, may hold values from -0.109375 to 0.109375
- weight_b: bfloat16 [3, 3, 3, 256, 512], replicated, may hold values from -0.078125 to 0.078125
- cotangent: bfloat16 [4, 64, 64, 512], P(None, 'space', 'tm'), may hold values from -6 to 6
Outputs:
- grad_features: bfloat16 [8, 128, 128, 128], P('tm', 'space')
- grad_wa: float32 [3, 3, 3, 128, 256], P(None, None, None, None, ('tm', 'space'))
- grad_wb: float32 [3, 3, 3, 256, 512], P(None, None, None, ('tm', 'space'))
The draws below stay inside these ranges and needn't reach their ends.
All inputs are finite; a program needn't handle non-finite values.
Results may differ from the reference program's by a relative error of at most 0.0075.
Values may be sent and summed in bfloat16 or wider, within the bound.
A program may use at most 128 MiB of HBM per device.

```python
import jax
import jax.numpy as jnp
from jax import lax

C_IN = 128
C_MID = 256
C_OUT = 512
WID = 128
FRAMES = 8
ROWS = 128


def block_levels(stream_key, shape, cuts, least, largest):
    def one(dim, blocks):
        heights = jax.random.uniform(jax.random.fold_in(jax.random.fold_in(stream_key, 6), dim), (blocks,), jnp.float32, least / len(cuts), largest / len(cuts))
        return jnp.repeat(jnp.exp(heights), shape[dim] // blocks).reshape((-1,) + (1,) * (len(shape) - dim - 1))

    gain = one(*cuts[0])
    for cut in cuts[1:]:
        gain = gain * one(*cut)
    return gain


def noise(key, shape, scale, limit, split=(), held_as=jnp.bfloat16):
    array = scale * jax.random.normal(key, shape, jnp.float32)
    if split:
        array = array * block_levels(key, shape, split, -0.22, 0.18)
    return jnp.clip(array, -limit, limit).astype(held_as)


def setup_inputs(seed: int = 0) -> dict:
    seeds = jax.random.split(jax.random.key(seed), 5)
    features = noise(seeds[0], (FRAMES, ROWS, WID, C_IN), 1.0, 6.0, ((0, 4), (1, 32)))
    weight_a = noise(seeds[1], (3, 3, 3, C_IN, C_MID), (27 * C_IN) ** -0.5, 0.109375)
    weight_b = noise(seeds[2], (3, 3, 3, C_MID, C_OUT), (27 * C_MID) ** -0.5, 0.078125)
    cotangent = noise(seeds[3], (FRAMES // 2, ROWS // 2, WID // 2, C_OUT), 1.0, 6.0, ((1, 32), (2, 4)))
    return {"features": features, "weight_a": weight_a, "weight_b": weight_b, "cotangent": cotangent}


def conv_same(field, weight):
    padded = jnp.pad(field.astype(jnp.float32), ((1, 1), (1, 1), (1, 1), (0, 0)))
    result = lax.conv_general_dilated(padded[None], weight.astype(jnp.float32), (1, 1, 1), 'VALID', dimension_numbers=('NDHWC', 'DHWIO', 'NDHWC'), precision=lax.Precision.HIGHEST)
    return result[0]

def flipped(weight):
    return jnp.swapaxes(weight[::-1, ::-1, ::-1], 3, 4)

def weight_grad(field, grad):
    padded = jnp.pad(field.astype(jnp.float32), ((1, 1), (1, 1), (1, 1), (0, 0)))
    grad_wide = grad.astype(jnp.float32)
    frames, height, width = (grad.shape[0], grad.shape[1], grad.shape[2])
    pieces = []
    for offset_t in range(3):
        for offset_h in range(3):
            for offset_w in range(3):
                window = padded[offset_t:offset_t + frames, offset_h:offset_h + height, offset_w:offset_w + width, :]
                pieces.append(lax.dot_general(window, grad_wide, (((0, 1, 2), (0, 1, 2)), ((), ())), precision=lax.Precision.HIGHEST))
    return jnp.stack(pieces).reshape(3, 3, 3, field.shape[3], grad.shape[3])

def reference(features, weight_a, weight_b, cotangent):
    preact = conv_same(features, weight_a)
    sigmoid_pre = jax.nn.sigmoid(preact)
    activated = preact * sigmoid_pre
    frames, height, width, channels = activated.shape
    pooled = activated.reshape(frames // 2, 2, height // 2, 2, width // 2, 2, channels).mean(axis=(1, 3, 5))
    pooled = pooled.astype(jnp.bfloat16)
    grad_wb = weight_grad(pooled, cotangent)
    grad_pooled = conv_same(cotangent, flipped(weight_b)).astype(jnp.bfloat16)
    small = grad_pooled.astype(jnp.float32)
    upsampled = jnp.broadcast_to(small[:, None, :, None, :, None, :], (frames // 2, 2, height // 2, 2, width // 2, 2, channels))
    upsampled = upsampled.reshape(frames, height, width, channels) / 8.0
    grad_pre = (upsampled * sigmoid_pre * (1.0 + preact * (1.0 - sigmoid_pre))).astype(jnp.bfloat16)
    grad_wa = weight_grad(features, grad_pre)
    grad_features = conv_same(grad_pre, flipped(weight_a)).astype(jnp.bfloat16)
    return (grad_features, grad_wa, grad_wb)
```

```python
import jax
import jax.numpy as jnp
from jax import lax
from jax.experimental import pallas as pl
from jax.experimental.pallas import tpu as pltpu
from jax.sharding import PartitionSpec as P

F32 = jnp.float32
BF16 = jnp.bfloat16
MESH = pl.DeviceIdType.MESH
TM = 4
SPACE = 32
ZG = 4
DIRS = [(dt, ds) for dt in (-1, 0, 1) for ds in (-1, 0, 1) if (dt, ds) != (0, 0)]
TAPS = [(a, b, c) for a in range(3) for b in range(3) for c in range(3)]
NT = (((1,), (1,)), ((), ()))


def dot(a, b):
    return lax.dot_general(a, b, (((1,), (0,)), ((), ())), preferred_element_type=F32)


def dot_nt(a, b):
    return lax.dot_general(a, b, NT, preferred_element_type=F32)


def valid(t, s, dt, ds):
    ok = jnp.bool_(True)
    if dt == 1:
        ok = t < TM - 1
    if dt == -1:
        ok = t > 0
    if ds == 1:
        ok = jnp.logical_and(ok, s < SPACE - 1)
    if ds == -1:
        ok = jnp.logical_and(ok, s > 0)
    return ok


def source_span(d, size):
    return (0, size) if d == 0 else ((size - 1, 1) if d == 1 else (0, 1))


def landing_span(d, size):
    return (1, size) if d == 0 else ((0, 1) if d == 1 else (size + 1, 1))


def shift_rows(x, step):
    rows = x.shape[0]
    index = lax.broadcasted_iota(jnp.int32, x.shape, 0)
    if step == 1:
        return jnp.where(index == 0, 0.0, pltpu.roll(x, 1, 0))
    return jnp.where(index == rows - 1, 0.0, pltpu.roll(x, rows - 1, 0))


def fill_edges(buf, t, s):
    @pl.when(t == 0)
    def _():
        buf[1, 0] = jnp.zeros(buf.shape[2:], BF16)

    @pl.when(t == TM - 1)
    def _():
        buf[1, 3] = jnp.zeros(buf.shape[2:], BF16)

    @pl.when(s == 0)
    def _():
        for f in range(4):
            buf[1, f, 0] = jnp.zeros(buf.shape[3:], BF16)

    @pl.when(s == SPACE - 1)
    def _():
        for f in range(4):
            buf[1, f, 5] = jnp.zeros(buf.shape[3:], BF16)


def fill_shifts(buf):
    def step(k, carry):
        f, r = (k // 6, lax.rem(k, 6))
        x = buf[1, f, r].astype(F32)
        buf[0, f, r] = shift_rows(x, 1).astype(BF16)
        buf[2, f, r] = shift_rows(x, -1).astype(BF16)
        return carry

    lax.fori_loop(0, 24, step, 0)


def body(
    feat, wa_hbm, wb_hbm, cot,
    gf_out, ga_out, gb_out,
    wa, wb, xs, cs, cw, col, colh, colf, gps, gpl, pre, pool, pt, pz, gs, gt, zz, outa, outb,
    sb, rb, pxs, pxr, sa, ra, tmp, pld,
    wsem, fs, fr, hs, hr, ws, wr, qs, qr, ps, pr, gsend, grecv, bs, br, xsend, xrecv, asend, arecv,
):
    t = lax.axis_index("tm")
    s = lax.axis_index("space")
    z = lax.rem(s, ZG)
    group = s - z
    core = lax.rem(t, 2)
    pair = t // 2

    def remote(src, dst, send, recv, tt, ss):
        return pltpu.make_async_remote_copy(
            src_ref=src, dst_ref=dst, send_sem=send, recv_sem=recv, device_id=(tt, ss), device_id_type=MESH
        )

    def wait_bytes(ref, sem):
        pltpu.make_async_copy(ref, ref, sem).wait()

    load_wa = pltpu.make_async_copy(wa_hbm, wa, wsem.at[0])
    load_wb = pltpu.make_async_copy(wb_hbm, wb, wsem.at[1])
    load_wb.start()
    load_wa.start()

    def halo_copy(source, target, base, d, send, recv):
        dt, ds = DIRS[d]
        f0, fn = source_span(dt, 2)
        r0, rn = source_span(ds, 4)
        lf, _ = landing_span(dt, 2)
        lr, _ = landing_span(ds, 4)
        return remote(
            source.at[pl.ds(base + f0, fn), pl.ds(base + r0, rn)],
            target.at[pl.ds(lf, fn), pl.ds(lr, rn)],
            send.at[d], recv.at[d], t + dt, s + ds,
        )

    for d in range(8):
        @pl.when(valid(t, s, *DIRS[d]))
        def _(d=d):
            halo_copy(feat, xs.at[1], 0, d, fs, fr).start()

    def cot_row(ds):
        r0, _ = source_span(ds, 2)
        lr, _ = landing_span(ds, 2)
        k = 0 if ds == -1 else 1
        return remote(
            cot.at[:, pl.ds(r0, 1)], cs.at[1, pl.ds(1, 4), pl.ds(lr, 1)], hs.at[k], hr.at[k], t, s + ds
        )

    for ds in (-1, 1):
        @pl.when(valid(t, s, 0, ds))
        def _(ds=ds):
            cot_row(ds).start()

    tmp[...] = jnp.zeros_like(tmp)
    for f in range(4):
        for r in range(2):
            x = cot[f, r].astype(F32)
            k = f * 2 + r
            tmp[0, pl.ds(k, 1), :] = x[0:1, :]
            tmp[1, pl.ds(k, 1), :] = x[15:16, :]
    col[...] = tmp[...].astype(BF16)

    def cot_col(dt, ds):
        side = 0 if dt == 1 else 1
        k = 2 + side * 3 + ds + 1
        return remote(
            col.at[1 if dt == 1 else 0], colh.at[side, 1 - ds], hs.at[k], hr.at[k], t + dt, s + ds
        )

    for dt in (-1, 1):
        for ds in (-1, 0, 1):
            @pl.when(valid(t, s, dt, ds))
            def _(dt=dt, ds=ds):
                cot_col(dt, ds).start()

    def gather_cot(j, tt, zd):
        return remote(
            cot.at[:, :, :, pl.ds(pl.multiple_of(zd * 128, 128), 128)],
            cw.at[z, :, :, pl.ds(pl.multiple_of(t * 16, 16), 16), :],
            ws.at[0 if j % 4 == 0 else 1], wr.at[0 if j % 4 == 0 else 1], tt, group + zd,
        )

    for j in range(1, 16):
        gather_cot(j, lax.rem(t + j // 4, TM), lax.rem(z + j % 4, ZG)).start()
    keep_cot = pltpu.make_async_copy(
        cot.at[:, :, :, pl.ds(pl.multiple_of(z * 128, 128), 128)],
        cw.at[z, :, :, pl.ds(pl.multiple_of(t * 16, 16), 16), :],
        wsem.at[2],
    )
    keep_cot.start()

    for f in range(2):
        for r in range(4):
            xs[1, 1 + f, 1 + r] = feat[f, r]
    fill_edges(xs, t, s)
    fill_edges(gs, t, s)
    for c in range(3):
        cs[c, 0] = jnp.zeros(cs.shape[2:], BF16)
        cs[c, 5] = jnp.zeros(cs.shape[2:], BF16)
    for f in range(4):
        for r in range(2):
            cs[1, 1 + f, 1 + r] = cot[f, r]

    @pl.when(t == 0)
    def _():
        colh[0] = jnp.zeros(colh.shape[1:], BF16)

    @pl.when(t == TM - 1)
    def _():
        colh[1] = jnp.zeros(colh.shape[1:], BF16)

    @pl.when(s == 0)
    def _():
        for side in range(2):
            colh[side, 0] = jnp.zeros(colh.shape[2:], BF16)
        for f in range(4):
            cs[1, 1 + f, 0] = jnp.zeros(cs.shape[3:], BF16)
        pz[pl.ds(0, 4)] = jnp.zeros((4,) + pz.shape[1:], BF16)

    @pl.when(s == SPACE - 1)
    def _():
        for side in range(2):
            colh[side, 2] = jnp.zeros(colh.shape[2:], BF16)
        for f in range(4):
            cs[1, 1 + f, 3] = jnp.zeros(cs.shape[3:], BF16)

    @pl.when(group == SPACE - ZG)
    def _():
        pz[pl.ds(20, 4)] = jnp.zeros((4,) + pz.shape[1:], BF16)

    @pl.when(jnp.logical_and(group == 0, s > 0))
    def _():
        pz[pl.ds(0, 4)] = jnp.zeros((4,) + pz.shape[1:], BF16)

    for k in range(27, 32):
        outb[pl.ds(k * 64, 64), :] = jnp.zeros((64, 128), F32)
        outa[pl.ds(k * 256, 256), :] = jnp.zeros((256, 128), F32)
    for k in range(4):
        zz[k, 0] = jnp.zeros(zz.shape[2:], BF16)
        zz[k, 5] = jnp.zeros(zz.shape[2:], BF16)

    for ds in (-1, 1):
        @pl.when(valid(t, s, 0, -ds))
        def _(ds=ds):
            cot_row(ds).wait_recv()
    for dt in (-1, 1):
        for ds in (-1, 0, 1):
            @pl.when(valid(t, s, -dt, -ds))
            def _(dt=dt, ds=ds):
                cot_col(dt, ds).wait_recv()
    colf[...] = colh[...].astype(F32)
    index = lax.broadcasted_iota(jnp.int32, (16, 512), 0)
    for f in range(4):
        for r in range(4):
            j = (0, 1, 1, 2)[r]
            k = f * 2 + (1, 0, 1, 0)[r]
            x = cs[1, 1 + f, r].astype(F32)
            left = colf[0, j, pl.ds(k, 1), :]
            right = colf[1, j, pl.ds(k, 1), :]
            cs[0, 1 + f, r] = jnp.where(index == 0, left, pltpu.roll(x, 1, 0)).astype(BF16)
            cs[2, 1 + f, r] = jnp.where(index == 15, right, pltpu.roll(x, 15, 0)).astype(BF16)
    load_wb.wait()
    acc = jnp.zeros((128, 256), F32)
    for n, (a, b, c) in enumerate(TAPS):
        lhs = cs[2 - c, pl.ds(2 - a, 4), pl.ds(2 - b, 2)].reshape(128, 512)
        acc = acc + dot_nt(lhs, wb[n])
    gps[...] = acc.reshape(4, 2, 16, 256).astype(BF16)

    def give_tile(k):
        tt = lax.rem(t + k, TM)
        return remote(
            gps.at[tt], gpl.at[:, pl.ds(pl.multiple_of(t * 16, 16), 16), :], qs.at[k - 1], qr.at[k - 1], tt, s
        )

    for k in range(1, TM):
        give_tile(k).start()
    gpl[:, pl.ds(pl.multiple_of(t * 16, 16), 16), :] = gps[t]

    for d in range(8):
        dt, ds = DIRS[d]

        @pl.when(valid(t, s, -dt, -ds))
        def _(d=d):
            halo_copy(feat, xs.at[1], 0, d, fs, fr).wait_recv()
    fill_shifts(xs)
    load_wa.wait()
    for f in range(2):
        total = jnp.zeros((512, 256), F32)
        for a in range(3):
            parts = [xs[c, f + a, pl.ds(b, 4)].reshape(512, 128) for b in range(3) for c in range(3)]
            total = total + dot(jnp.concatenate(parts, axis=1), wa[pl.ds(a * 1152, 1152), :])
        pre[pl.ds(f * 512, 512), :] = total
    for q in range(2):
        summed = jnp.zeros((128, 256), F32)
        for f in range(2):
            for r in range(2):
                rows = pl.ds((f * 4 + q * 2 + r) * 128, 128)
                p = pre[rows, :]
                sig = jax.nn.sigmoid(p)
                summed = summed + p * sig
                pre[rows, :] = sig * (1.0 + p * (1.0 - sig))
        for lane in range(2):
            pool[lane] = summed[:, lane * 128 : lane * 128 + 128]
        for lane in range(2):
            even = pool[lane, pl.ds(0, 64, stride=2), :]
            odd = pool[lane, pl.ds(1, 64, stride=2), :]
            pld[lane, pl.ds(q * 64, 64), :] = (even + odd) * 0.125
    for lane in range(2):
        turned = pld[lane].T.astype(BF16)
        pt[2 * lane] = turned[0:64]
        pt[2 * lane + 1] = turned[64:128]

    def give_pooled(tt, ss, slot, k):
        return remote(pt.at[tt], pz.at[slot * 4 + t], ps.at[k], pr.at[k], tt, ss)

    for j in range(1, 16):
        give_pooled(lax.rem(t + j // 4, TM), group + lax.rem(z + j % 4, ZG), z + 1, 0).start()
    pz[(z + 1) * 4 + t] = pt[t]

    @pl.when(jnp.logical_and(z == 0, s > 0))
    def _():
        for j in range(16):
            give_pooled(lax.rem(t + j // 4, TM), group - ZG + j % 4, 5, 1).start()

    @pl.when(jnp.logical_and(z == ZG - 1, s < SPACE - 1))
    def _():
        for j in range(16):
            give_pooled(lax.rem(t + j // 4, TM), group + ZG + j % 4, 0, 2).start()

    for k in range(1, TM):
        give_tile(k).wait_recv()
    for q in range(2):
        u = gpl[q].astype(F32) * 0.125
        for lane in range(2):
            half = u[:, lane * 128 : lane * 128 + 128]
            pool[lane, pl.ds(0, 64, stride=2), :] = half
            pool[lane, pl.ds(1, 64, stride=2), :] = half
        for f in range(2):
            for r in range(2):
                k = f * 4 + q * 2 + r
                for lane in range(2):
                    g = pool[lane] * pre[pl.ds(k * 128, 128), pl.ds(lane * 128, 128)]
                    gs[1, 1 + f, 1 + q * 2 + r, :, pl.ds(lane * 128, 128)] = g.astype(BF16)
                    gt[pl.ds(lane * 128, 128), pl.ds(k * 128, 128)] = g.T.astype(BF16)
    for d in range(8):
        @pl.when(valid(t, s, *DIRS[d]))
        def _(d=d):
            halo_copy(gs.at[1], gs.at[1], 1, d, gsend, grecv).start()

    def term(ab, carry):
        a, b = (ab // 3, lax.rem(ab, 3))
        rhs = jnp.concatenate([xs[c, pl.ds(a, 2), pl.ds(b, 4)].reshape(1024, 128) for c in range(3)], axis=1)
        res = dot(gt[...], rhs)
        for c in range(3):
            outa[pl.ds(pl.multiple_of((ab * 3 + c) * 256, 256), 256), :] = res[:, c * 128 : c * 128 + 128]
        return carry

    lax.fori_loop(0, 9, term, 0)

    def pick_a(o):
        return jnp.concatenate([outa[pl.ds(o, 32, stride=256), :], outa[pl.ds(o + 1, 32, stride=256), :]], axis=0)

    partner = t + 1 - 2 * core

    def give_pair(y):
        rows = pl.ds(y * 32, 32)
        return remote(pxs.at[rows], pxr.at[rows], xsend.at[y], xrecv.at[y], partner, s)

    for y in range(2):
        def cut(k, carry, y=y):
            pxs[y * 32 + k] = pick_a((1 - core + 2 * y) * 64 + 2 * k).astype(BF16)
            return carry

        lax.fori_loop(0, 32, cut, 0)
        give_pair(y).start()

    wait_bytes(cw.at[0, :, :, pl.ds(0, 48), :], wr.at[0])
    wait_bytes(cw.at[pl.ds(0, 3)], wr.at[1])
    keep_cot.wait()
    wait_bytes(pz.at[pl.ds(0, 15)], pr.at[0])

    @pl.when(group > 0)
    def _():
        wait_bytes(pz.at[pl.ds(0, 4)], pr.at[2])

    @pl.when(group < SPACE - ZG)
    def _():
        wait_bytes(pz.at[pl.ds(0, 4)], pr.at[1])

    lane_id = lax.broadcasted_iota(jnp.int32, (64, 128), 1)
    low = lane_id < 64
    first = lax.rem(lane_id, 64) == 0
    last = lax.rem(lane_id, 64) == 63

    def spread(k, carry):
        block, f = (k // 4, lax.rem(k, 4))
        own = pz[(block + 1) * 4 + f].astype(F32)
        before = pltpu.roll(pz[block * 4 + f].astype(F32), 64, 1)
        after = pltpu.roll(pz[(block + 2) * 4 + f].astype(F32), 64, 1)
        turned = pltpu.roll(own, 64, 1)
        rows = [jnp.where(low, before, turned), own, jnp.where(low, turned, after)]
        for b in range(3):
            x = rows[b]
            cols = [jnp.where(first, 0.0, pltpu.roll(x, 1, 1)), x, jnp.where(last, 0.0, pltpu.roll(x, 127, 1))]
            for c in range(3):
                zz[block, 1 + f, pl.ds((b * 3 + c) * 64, 64), :] = cols[c].astype(BF16)
        return carry

    lax.fori_loop(0, 16, spread, 0)
    for a in range(3):
        lhs = jnp.concatenate([zz[block, f + a] for block in range(4) for f in range(4)], axis=1)
        outb[pl.ds(a * 576, 576), :] = dot(lhs, cw[...].reshape(2048, 128))

    def share_b(j, carry):
        ss = lax.rem(s + j, SPACE)
        o = 2 * ss
        piece = jnp.concatenate([outb[pl.ds(o, 32, stride=64), :], outb[pl.ds(o + 1, 32, stride=64), :]], axis=0)
        sb[ss] = piece.astype(BF16)

        @pl.when(j > 0)
        def _():
            remote(sb.at[ss], rb.at[s], bs, br, t, ss).start()

        return carry

    lax.fori_loop(0, SPACE, share_b, 0)
    rb[s] = sb[s]

    for y in range(2):
        give_pair(y).wait_recv()
    slot = pair * 32 + s

    def share_a(j, carry):
        y = lax.rem(pair + j // 32, 2)
        ss = lax.rem(s + j, SPACE)
        tt = core + 2 * y
        k = y * 32 + ss
        sa[k] = (pick_a(tt * 64 + 2 * ss) + pxr[k].astype(F32)).astype(BF16)

        @pl.when(j > 0)
        def _():
            remote(sa.at[k], ra.at[slot], asend, arecv, tt, ss).start()

        return carry

    lax.fori_loop(0, 64, share_a, 0)
    ra[slot] = sa[slot]

    for d in range(8):
        dt, ds = DIRS[d]

        @pl.when(valid(t, s, -dt, -ds))
        def _(d=d):
            halo_copy(gs.at[1], gs.at[1], 1, d, gsend, grecv).wait_recv()
    fill_shifts(gs)
    for f in range(2):
        total = jnp.zeros((512, 128), F32)
        for a in range(3):
            for b in range(3):
                lhs = jnp.concatenate(
                    [gs[2 - c, f + 2 - a, pl.ds(2 - b, 4)].reshape(512, 256) for c in range(3)], axis=1
                )
                rhs = jnp.concatenate(
                    [wa[pl.ds(((a * 3 + b) * 3 + c) * 128, 128), :] for c in range(3)], axis=1
                )
                total = total + dot_nt(lhs, rhs)
        gf_out[f] = total.reshape(4, 128, 128).astype(BF16)

    wait_bytes(rb.at[pl.ds(0, 31)], br)
    for k in range(4):
        def add_b(g, total, k=k):
            return total + rb[g * 4 + k].astype(F32)

        gb_out[k] = lax.fori_loop(0, 8, add_b, jnp.zeros((64, 128), F32))
    wait_bytes(ra.at[pl.ds(0, 63)], arecv)
    ga_out[...] = lax.fori_loop(0, 64, lambda k, total: total + ra[k].astype(F32), jnp.zeros((64, 128), F32))

    for d in range(8):
        @pl.when(valid(t, s, *DIRS[d]))
        def _(d=d):
            halo_copy(feat, xs.at[1], 0, d, fs, fr).wait_send()
            halo_copy(gs.at[1], gs.at[1], 1, d, gsend, grecv).wait_send()
    for ds in (-1, 1):
        @pl.when(valid(t, s, 0, ds))
        def _(ds=ds):
            cot_row(ds).wait_send()
    for dt in (-1, 1):
        for ds in (-1, 0, 1):
            @pl.when(valid(t, s, dt, ds))
            def _(dt=dt, ds=ds):
                cot_col(dt, ds).wait_send()
    wait_bytes(cw.at[0, :, :, pl.ds(0, 48), :], ws.at[0])
    wait_bytes(cw.at[pl.ds(0, 3)], ws.at[1])
    for k in range(1, TM):
        give_tile(k).wait_send()
    wait_bytes(pz.at[pl.ds(0, 15)], ps.at[0])

    @pl.when(jnp.logical_and(z == 0, s > 0))
    def _():
        wait_bytes(pz.at[pl.ds(0, 16)], ps.at[1])

    @pl.when(jnp.logical_and(z == ZG - 1, s < SPACE - 1))
    def _():
        wait_bytes(pz.at[pl.ds(0, 16)], ps.at[2])

    for y in range(2):
        give_pair(y).wait_send()
    wait_bytes(rb.at[pl.ds(0, 31)], bs)
    wait_bytes(ra.at[pl.ds(0, 63)], asend)


def shards(features, weight_a, weight_b, cotangent):
    vmem = pl.BlockSpec(memory_space=pltpu.VMEM)
    far = pl.BlockSpec(memory_space=pl.ANY)
    dma = pltpu.SemaphoreType.DMA
    gf, ga, gb = pl.pallas_call(
        body,
        out_shape=(
            jax.ShapeDtypeStruct((2, 4, 128, 128), BF16),
            jax.ShapeDtypeStruct((64, 128), F32),
            jax.ShapeDtypeStruct((4, 64, 128), F32),
        ),
        in_specs=[vmem, far, far, vmem],
        out_specs=(vmem, vmem, vmem),
        scratch_shapes=[
            pltpu.VMEM((3456, 256), BF16),
            pltpu.VMEM((27, 256, 512), BF16),
            pltpu.VMEM((3, 4, 6, 128, 128), BF16),
            pltpu.VMEM((3, 6, 4, 16, 512), BF16),
            pltpu.VMEM((4, 4, 2, 64, 128), BF16),
            pltpu.VMEM((2, 16, 512), BF16),
            pltpu.VMEM((2, 3, 16, 512), BF16),
            pltpu.VMEM((2, 3, 16, 512), F32),
            pltpu.VMEM((4, 2, 16, 256), BF16),
            pltpu.VMEM((2, 64, 256), BF16),
            pltpu.VMEM((1024, 256), F32),
            pltpu.VMEM((2, 128, 128), F32),
            pltpu.VMEM((4, 64, 128), BF16),
            pltpu.VMEM((24, 64, 128), BF16),
            pltpu.VMEM((3, 4, 6, 128, 256), BF16),
            pltpu.VMEM((256, 1024), BF16),
            pltpu.VMEM((4, 6, 576, 128), BF16),
            pltpu.VMEM((8192, 128), F32),
            pltpu.VMEM((2048, 128), F32),
            pltpu.VMEM((32, 64, 128), BF16),
            pltpu.VMEM((32, 64, 128), BF16),
            pltpu.VMEM((64, 64, 128), BF16),
            pltpu.VMEM((64, 64, 128), BF16),
            pltpu.VMEM((64, 64, 128), BF16),
            pltpu.VMEM((64, 64, 128), BF16),
            pltpu.VMEM((2, 16, 512), F32),
            pltpu.VMEM((2, 128, 128), F32),
            dma((3,)), dma((8,)), dma((8,)), dma((8,)), dma((8,)), dma((2,)), dma((2,)),
            dma((3,)), dma((3,)), dma((3,)), dma((3,)), dma((8,)), dma((8,)),
            dma, dma, dma((2,)), dma((2,)), dma, dma,
        ],
        compiler_params=pltpu.CompilerParams(has_side_effects=True, vmem_limit_bytes=56 * 2**20),
    )(features, weight_a.reshape(3456, 256), weight_b.reshape(27, 256, 512), cotangent)
    grad_wa = ga.reshape(2, 32, 128)[:, :27].transpose(1, 2, 0).reshape(3, 3, 3, 128, 2)
    grad_wb = gb.reshape(4, 2, 32, 128)[:, :, :27].transpose(2, 1, 0, 3).reshape(3, 3, 3, 2, 512)
    return (gf, grad_wa, grad_wb)


def solution(mesh):
    placed = (P("tm", "space", None, None), P(), P(), P(None, "space", "tm", None))
    return jax.shard_map(
        shards,
        mesh=mesh,
        in_specs=placed,
        out_specs=(
            P("tm", "space", None, None),
            P(None, None, None, None, ("tm", "space")),
            P(None, None, None, ("tm", "space"), None),
        ),
        check_vma=False,
    )
```

```python
import jax
import jax.numpy as jnp
from jax import lax
from jax.experimental import pallas as pl
from jax.experimental.pallas import tpu as pltpu
from jax.sharding import PartitionSpec as P

F32 = jnp.float32
BF16 = jnp.bfloat16
MESH = pl.DeviceIdType.MESH
TM = 4
SPACE = 32
ZG = 4
SIDES = [(-1, 0), (1, 0), (0, -1), (0, 1)]
CORNERS = [(dt, ds) for dt in (-1, 1) for ds in (-1, 1)]
TAPS = [(a, b, c) for a in range(3) for b in range(3) for c in range(3)]
NT = (((1,), (1,)), ((), ()))


def dot(a, b):
    return lax.dot_general(a, b, (((1,), (0,)), ((), ())), preferred_element_type=F32)


def dot_nt(a, b):
    return lax.dot_general(a, b, NT, preferred_element_type=F32)


def valid(t, s, dt, ds):
    ok = jnp.bool_(True)
    if dt == 1:
        ok = t < TM - 1
    if dt == -1:
        ok = t > 0
    if ds == 1:
        ok = jnp.logical_and(ok, s < SPACE - 1)
    if ds == -1:
        ok = jnp.logical_and(ok, s > 0)
    return ok


def source_span(d, size):
    return (0, size) if d == 0 else ((size - 1, 1) if d == 1 else (0, 1))


def landing_span(d, size):
    return (1, size) if d == 0 else ((0, 1) if d == 1 else (size + 1, 1))


def shift_rows(x, step):
    rows = x.shape[0]
    index = lax.broadcasted_iota(jnp.int32, x.shape, 0)
    if step == 1:
        return jnp.where(index == 0, 0.0, pltpu.roll(x, 1, 0))
    return jnp.where(index == rows - 1, 0.0, pltpu.roll(x, rows - 1, 0))


def fill_edges(buf, t, s):
    @pl.when(t == 0)
    def _():
        buf[1, 0] = jnp.zeros(buf.shape[2:], BF16)

    @pl.when(t == TM - 1)
    def _():
        buf[1, 3] = jnp.zeros(buf.shape[2:], BF16)

    @pl.when(s == 0)
    def _():
        for f in range(4):
            buf[1, f, 0] = jnp.zeros(buf.shape[3:], BF16)

    @pl.when(s == SPACE - 1)
    def _():
        for f in range(4):
            buf[1, f, 5] = jnp.zeros(buf.shape[3:], BF16)


def fill_shifts(buf, own):
    def shift(f, r):
        x = buf[1, f, r].astype(F32)
        buf[0, f, r] = shift_rows(x, 1).astype(BF16)
        buf[2, f, r] = shift_rows(x, -1).astype(BF16)

    def inner(k, carry):
        shift(1 + k // 4, 1 + lax.rem(k, 4))
        return carry

    def frames(k, carry):
        shift(3 * (k // 6), lax.rem(k, 6))
        return carry

    def rows(k, carry):
        shift(1 + k // 2, 5 * lax.rem(k, 2))
        return carry

    if own:
        lax.fori_loop(0, 8, inner, 0)
    else:
        lax.fori_loop(0, 12, frames, 0)
        lax.fori_loop(0, 4, rows, 0)


def body(
    feat, wa_hbm, wb_hbm, cot,
    gf_out, ga_out, gb_out,
    wa, wb, xs, cs, cw, col, colh, colf, gps, gpl, pre, pool, pt, pz, gs, gt, zz, outa, outb,
    sb, rb, pxs, pxr, su, a1, r1, t1, a2, r2, tmp, pld, edge, edges, fin, ct, ya, wt,
    wsem, fs, fr, hs, hr, ws, wr, qs, qr, ps, pr, gsend, grecv, bs, br, xsend, xrecv, asend, arecv,
):
    t = lax.axis_index("tm")
    s = lax.axis_index("space")
    z = lax.rem(s, ZG)
    group = s - z
    core = lax.rem(t, 2)
    pair = t // 2

    def remote(src, dst, send, recv, tt, ss):
        return pltpu.make_async_remote_copy(
            src_ref=src, dst_ref=dst, send_sem=send, recv_sem=recv, device_id=(tt, ss), device_id_type=MESH
        )

    def wait_bytes(ref, sem):
        pltpu.make_async_copy(ref, ref, sem).wait()

    load_wa = pltpu.make_async_copy(wa_hbm, wa, wsem.at[0])
    load_wb = pltpu.make_async_copy(wb_hbm, wb, wsem.at[1])
    keep_tile = pltpu.make_async_copy(cot, cs.at[1, pl.ds(1, 4), pl.ds(1, 2)], wsem.at[3])
    keep_feat = pltpu.make_async_copy(feat, xs.at[1, pl.ds(1, 2), pl.ds(1, 4)], wsem.at[4])
    keep_tile.start()
    keep_feat.start()
    load_wa.start()
    load_wb.start()

    barrier = pltpu.get_barrier_semaphore()

    def greet(tt, ss):
        pl.semaphore_signal(barrier, inc=1, device_id=(tt, ss), device_id_type=MESH)

    def greet_near(j, carry):
        ss = group - ZG + lax.rem(j, 12)

        @pl.when(jnp.logical_and(ss >= 0, ss < SPACE))
        def _():
            greet(1 - core + 2 * (j // 12), ss)

        return carry

    def greet_far(j, carry):
        @pl.when(j > 0)
        def _():
            greet(core + 2 * lax.rem(pair + j // 32, 2), lax.rem(s + j, SPACE))

        return carry

    lax.fori_loop(0, 24, greet_near, 0)
    lax.fori_loop(0, 64, greet_far, 0)
    greeted = 63 + 24 - jnp.where(group == 0, 8, 0) - jnp.where(group == SPACE - ZG, 8, 0)

    pl.semaphore_wait(barrier, greeted)

    lane_id = lax.broadcasted_iota(jnp.int32, (64, 128), 1)
    low = lane_id < 64
    first = lax.rem(lane_id, 64) == 0
    last = lax.rem(lane_id, 64) == 63

    def halo_copy(source, target, base, d, send, recv):
        dt, ds = SIDES[d]
        f0, fn = source_span(dt, 2)
        r0, rn = source_span(ds, 4)
        lf, _ = landing_span(dt, 2)
        lr, _ = landing_span(ds, 4)
        return remote(
            source.at[pl.ds(base + f0, fn), pl.ds(base + r0, rn)],
            target.at[pl.ds(lf, fn), pl.ds(lr, rn)],
            send.at[d], recv.at[d], t + dt, s + ds,
        )

    def halo_wait(source, target, base, ways, send, recv):
        for d in ways:
            dt, ds = SIDES[d]

            @pl.when(valid(t, s, -dt, -ds))
            def _(d=d):
                halo_copy(source, target, base, d, send, recv).wait_recv()

    def corner_copy(target, d, send, recv):
        dt, ds = CORNERS[d]
        row = pl.ds(0 if ds == 1 else 5, 1)
        return remote(
            target.at[pl.ds(2 if dt == 1 else 1, 1), row],
            target.at[pl.ds(0 if dt == 1 else 3, 1), row],
            send.at[4 + d], recv.at[4 + d], t + dt, s,
        )

    def corner_valid(d, arriving):
        dt, ds = CORNERS[d]
        return jnp.logical_and(valid(t, s, -dt if arriving else dt, 0), valid(t, s, 0, -ds))

    def corners(target, send, recv, what):
        for d in range(4):
            @pl.when(corner_valid(d, what == "recv"))
            def _(d=d):
                copy = corner_copy(target, d, send, recv)
                if what == "start":
                    copy.start()
                elif what == "recv":
                    copy.wait_recv()
                else:
                    copy.wait_send()

    for d in range(4):
        @pl.when(valid(t, s, *SIDES[d]))
        def _(d=d):
            halo_copy(feat, xs.at[1], 0, d, fs, fr).start()

    def cot_row(ds):
        r0, _ = source_span(ds, 2)
        lr, _ = landing_span(ds, 2)
        k = 0 if ds == -1 else 1
        return remote(
            cot.at[:, pl.ds(r0, 1)], cs.at[1, pl.ds(1, 4), pl.ds(lr, 1)], hs.at[k], hr.at[k], t, s + ds
        )

    for ds in (-1, 1):
        @pl.when(valid(t, s, 0, ds))
        def _(ds=ds):
            cot_row(ds).start()

    keep_tile.wait()
    tmp[...] = jnp.zeros_like(tmp)
    for f in range(4):
        for r in range(2):
            x = cs[1, 1 + f, 1 + r].astype(F32)
            k = f * 2 + r
            tmp[0, pl.ds(k, 1), :] = x[0:1, :]
            tmp[1, pl.ds(k, 1), :] = x[15:16, :]
    col[...] = tmp[...].astype(BF16)

    def cot_col(dt, ds):
        side = 0 if dt == 1 else 1
        k = 2 + side * 3 + ds + 1
        return remote(
            col.at[1 if dt == 1 else 0], colh.at[side, 1 - ds], hs.at[k], hr.at[k], t + dt, s + ds
        )

    for dt in (-1, 1):
        for ds in (-1, 0, 1):
            @pl.when(valid(t, s, dt, ds))
            def _(dt=dt, ds=ds):
                cot_col(dt, ds).start()

    def gather_cot(j, tt, zd):
        return remote(
            cot.at[:, :, :, pl.ds(pl.multiple_of(zd * 128, 128), 128)],
            cw.at[z, :, :, pl.ds(pl.multiple_of(t * 16, 16), 16), :],
            ws.at[0 if j == 4 else 1], wr.at[0 if j == 4 else 1], tt, group + zd,
        )

    for j in range(1, 8):
        gather_cot(j, core + 2 * lax.rem(pair + j // 4, 2), lax.rem(z + j % 4, ZG)).start()
    keep_cot = pltpu.make_async_copy(
        cot.at[:, :, :, pl.ds(pl.multiple_of(z * 128, 128), 128)],
        cw.at[z, :, :, pl.ds(pl.multiple_of(t * 16, 16), 16), :],
        wsem.at[2],
    )
    keep_cot.start()

    fill_edges(xs, t, s)
    fill_edges(gs, t, s)
    @pl.when(t == 0)
    def _():
        colh[0] = jnp.zeros(colh.shape[1:], BF16)

    @pl.when(t == TM - 1)
    def _():
        colh[1] = jnp.zeros(colh.shape[1:], BF16)

    @pl.when(s == 0)
    def _():
        for side in range(2):
            colh[side, 0] = jnp.zeros(colh.shape[2:], BF16)
        for f in range(4):
            cs[1, 1 + f, 0] = jnp.zeros(cs.shape[3:], BF16)

    @pl.when(s == SPACE - 1)
    def _():
        for side in range(2):
            colh[side, 2] = jnp.zeros(colh.shape[2:], BF16)
        for f in range(4):
            cs[1, 1 + f, 3] = jnp.zeros(cs.shape[3:], BF16)

    @pl.when(group == SPACE - ZG)
    def _():
        edges[1] = jnp.zeros(edges.shape[1:], BF16)

    @pl.when(group == 0)
    def _():
        edges[0] = jnp.zeros(edges.shape[1:], BF16)

    t1[...] = jnp.zeros_like(t1)
    for k in range(27, 32):
        outb[pl.ds(k * 64, 64), :] = jnp.zeros((64, 128), F32)
    for k in range(4):
        zz[k, 0] = jnp.zeros(zz.shape[2:], BF16)
        zz[k, 5] = jnp.zeros(zz.shape[2:], BF16)

    load_wa.wait()
    for n in range(27):
        wt[pl.ds(n * 256, 256), :] = wa[pl.ds(n * 128, 128), :].astype(F32).T.astype(BF16)
    keep_feat.wait()
    fill_shifts(xs, True)
    for ds in (-1, 1):
        @pl.when(valid(t, s, 0, -ds))
        def _(ds=ds):
            cot_row(ds).wait_recv()
    for dt in (-1, 1):
        for ds in (-1, 0, 1):
            @pl.when(valid(t, s, -dt, -ds))
            def _(dt=dt, ds=ds):
                cot_col(dt, ds).wait_recv()
    halo_wait(feat, xs.at[1], 0, (2, 3), fs, fr)
    corners(xs.at[1], fs, fr, "start")
    colf[...] = colh[...].astype(F32)
    index = lax.broadcasted_iota(jnp.int32, (16, 512), 0)
    for f in range(4):
        for r in range(4):
            j = (0, 1, 1, 2)[r]
            k = f * 2 + (1, 0, 1, 0)[r]
            x = cs[1, 1 + f, r].astype(F32)
            left = colf[0, j, pl.ds(k, 1), :]
            right = colf[1, j, pl.ds(k, 1), :]
            cs[0, 1 + f, r] = jnp.where(index == 0, left, pltpu.roll(x, 1, 0)).astype(BF16)
            cs[2, 1 + f, r] = jnp.where(index == 15, right, pltpu.roll(x, 15, 0)).astype(BF16)
    load_wb.wait()
    for b in range(3):
        for c in range(3):
            tile = cs[2 - c, pl.ds(1, 4), pl.ds(2 - b, 2)].reshape(128, 512)
            ct[pl.ds((b * 3 + c) * 512, 512), :] = tile.astype(F32).T.astype(BF16)
    for a in range(3):
        ya[a] = dot(jnp.concatenate([wb[a * 9 + n] for n in range(9)], axis=1), ct[...])
    cell = lax.broadcasted_iota(jnp.int32, (256, 128), 1)
    later = jnp.where(cell < 96, pltpu.roll(ya[0], 96, 1), 0.0)
    earlier = jnp.where(cell >= 32, pltpu.roll(ya[2], 32, 1), 0.0)
    gps[...] = (ya[1] + later + earlier).T.reshape(4, 2, 16, 256).astype(BF16)

    partner = t + 1 - 2 * core

    def forward_cot(y):
        part = cw.at[:, :, :, pl.ds(pl.multiple_of((core + 2 * y) * 16, 16), 16), :]
        return remote(part, part, ws.at[2 + y], wr.at[2 + y], partner, s)

    def give_tile(k):
        tt = lax.rem(t + k, TM)
        return remote(
            gps.at[tt], gpl.at[:, pl.ds(pl.multiple_of(t * 16, 16), 16), :], qs.at[k - 1], qr.at[k - 1], tt, s
        )

    for k in range(1, TM):
        give_tile(k).start()
    gpl[:, pl.ds(pl.multiple_of(t * 16, 16), 16), :] = gps[t]
    wait_bytes(cw.at[0, :, :, pl.ds(0, 16), :], wr.at[0])
    wait_bytes(cw.at[pl.ds(0, 3), :, :, pl.ds(0, 32), :], wr.at[1])
    keep_cot.wait()
    for y in range(2):
        forward_cot(y).start()

    halo_wait(feat, xs.at[1], 0, (0, 1), fs, fr)
    corners(xs.at[1], fs, fr, "recv")
    fill_shifts(xs, False)
    for f in range(2):
        parts = [xs[c, f + a, pl.ds(b, 4)].reshape(512, 128) for a, b, c in TAPS]
        pre[pl.ds(f * 512, 512), :] = dot(jnp.concatenate(parts, axis=1), wa[...])
    for q in range(2):
        summed = jnp.zeros((128, 256), F32)
        for f in range(2):
            for r in range(2):
                rows = pl.ds((f * 4 + q * 2 + r) * 128, 128)
                p = pre[rows, :]
                sig = jax.nn.sigmoid(p)
                summed = summed + p * sig
                pre[rows, :] = sig * (1.0 + p * (1.0 - sig))
        for lane in range(2):
            pool[lane] = summed[:, lane * 128 : lane * 128 + 128]
        for lane in range(2):
            even = pool[lane, pl.ds(0, 64, stride=2), :]
            odd = pool[lane, pl.ds(1, 64, stride=2), :]
            pld[lane, pl.ds(q * 64, 64), :] = (even + odd) * 0.125
    for lane in range(2):
        turned = pld[lane].astype(BF16).astype(F32).T
        for half in range(2):
            block = turned[half * 64 : half * 64 + 64]
            pt[2 * lane + half] = block.astype(BF16)
            top, bottom = (block[0:32], block[32:64])
            edge[0, 2 * lane + half] = jnp.where(low[0:32], top, pltpu.roll(bottom, 64, 1)).astype(BF16)
            edge[1, 2 * lane + half] = jnp.where(low[0:32], pltpu.roll(top, 64, 1), bottom).astype(BF16)

    def give_pooled(tt, ss):
        return remote(pt.at[tt], pz.at[(z + 1) * 4 + t], ps.at[0], pr.at[0], tt, ss)

    def give_edge(tt, ss, k):
        return remote(edge.at[k, tt], edges.at[1 - k, t], ps.at[1 + k], pr.at[2 - k], tt, ss)

    for j in range(1, 16):
        give_pooled(lax.rem(t + j // 4, TM), group + lax.rem(z + j % 4, ZG)).start()
    pz[(z + 1) * 4 + t] = pt[t]

    for k, inside, ss in ((0, jnp.logical_and(z == 0, s > 0), s - 1), (1, jnp.logical_and(z == ZG - 1, s < SPACE - 1), s + 1)):
        @pl.when(inside)
        def _(k=k, ss=ss):
            for j in range(1, TM):
                give_edge(lax.rem(t + j, TM), ss, k).start()
            give_edge(t, ss, k).start()

    for k in range(1, TM):
        give_tile(k).wait_recv()
    for q in range(2):
        u = gpl[q].astype(F32) * 0.125
        for lane in range(2):
            half = u[:, lane * 128 : lane * 128 + 128]
            pool[lane, pl.ds(0, 64, stride=2), :] = half
            pool[lane, pl.ds(1, 64, stride=2), :] = half
        for f in range(2):
            for r in range(2):
                k = f * 4 + q * 2 + r
                for lane in range(2):
                    g = pool[lane] * pre[pl.ds(k * 128, 128), pl.ds(lane * 128, 128)]
                    gs[1, 1 + f, 1 + q * 2 + r, :, pl.ds(lane * 128, 128)] = g.astype(BF16)
                    gt[pl.ds(lane * 128, 128), pl.ds(k * 128, 128)] = g.T.astype(BF16)
    for d in range(4):
        @pl.when(valid(t, s, *SIDES[d]))
        def _(d=d):
            halo_copy(gs.at[1], gs.at[1], 1, d, gsend, grecv).start()

    def pass_edge(k, zd):
        return remote(edges.at[k], edges.at[k], ps.at[3 + k], pr.at[1 + k], t, group + zd)

    for k, passes in ((0, jnp.logical_and(z == 0, s > 0)), (1, jnp.logical_and(z == ZG - 1, s < SPACE - 1))):
        @pl.when(passes)
        def _(k=k):
            wait_bytes(edges.at[k], pr.at[1 + k])
            for j in range(1, ZG):
                pass_edge(k, lax.rem(z + j, ZG)).start()


    def give_pair(m):
        taps = pl.ds(m * 9, 9)
        return remote(pxs.at[taps], pxr.at[taps], xsend.at[m], xrecv.at[m], partner, s)

    def term(ab, carry):
        a, b = (ab // 3, lax.rem(ab, 3))
        rhs = jnp.concatenate([xs[c, pl.ds(a, 2), pl.ds(b, 4)].reshape(1024, 128) for c in range(3)], axis=1)
        res = dot(gt[...], rhs)
        for c in range(3):
            n = ab * 3 + c
            base = n * 256
            outa[pl.ds(pl.multiple_of(base, 256), 256), :] = res[:, c * 128 : c * 128 + 128]
            for y in range(2):
                other = pl.multiple_of(base + (1 - core + 2 * y) * 64, 64)
                pxs[n, y] = outa[pl.ds(other, 64), :].astype(BF16)
        return carry

    for m in range(3):
        lax.fori_loop(m * 3, m * 3 + 3, term, 0)
        give_pair(m).start()
    halo_wait(gs.at[1], gs.at[1], 1, (2, 3), gsend, grecv)
    corners(gs.at[1], gsend, grecv, "start")
    fill_shifts(gs, True)

    sx, sy, sz = (s // 8, 2 * lax.rem(s // 4, 2) + pair, z)

    def place(x, y, zed):
        return (core + 2 * lax.rem(y, 2), x * 8 + (y // 2) * 4 + zed)

    coord = (sx, sy, sz)
    for m in range(3):
        give_pair(m).wait_recv()

        def add_pair(i, carry, m=m):
            n = m * 9 + i
            for y in range(2):
                own = pl.multiple_of(n * 256 + (core + 2 * y) * 64, 64)
                su[y] = outa[pl.ds(own, 64), :] + pxr[n, y].astype(F32)
            for v in range(4):
                if m == 0:
                    rows = [su[y, pl.ds(v * 16, 16), :] for y in range(2)]
                elif m == 1:
                    rows = [su[v % 2, pl.ds(x * 16 + (v // 2) * 8, 8), :] for x in range(4)]
                else:
                    rows = [su[y, pl.ds(v * 2 + e, 8, stride=8), :] for y in range(2) for e in range(2)]
                at = pl.ds(pl.multiple_of(i * 32, 32), 32)
                a1[m, v, at, :] = jnp.concatenate(rows, axis=0).astype(BF16)
            return carry

        lax.fori_loop(0, 9, add_pair, 0)
        for k in range(1, 4):
            v = lax.rem(coord[m] + k, 4)
            to = [sx, sy, sz]
            to[m] = v
            remote(a1.at[m, v], r1.at[m, coord[m]], asend.at[m], arecv.at[m], *place(*to)).start()
        r1[m, coord[m]] = a1[m, coord[m]]

    w2 = (pair * 8 + lax.rem(s, 8), sx * 4 + sz, pair * 8 + s // 4)

    def second(m):
        wait_bytes(r1.at[m, pl.ds(0, 3)], arecv.at[m])
        total = r1[m, 0].astype(F32)
        for k in range(1, 4):
            total = total + r1[m, k].astype(F32)
        t1[pl.ds(0, 288), :] = total

        def share_a(j, carry):
            d = lax.rem(w2[m] + j, 16)
            if m == 0:
                q, step, tt, ss = (d * 2, 1, core + 2 * (d // 8), sx * 8 + lax.rem(d, 8))
            elif m == 1:
                q, step, tt, ss = (d * 2, 1, t, (d // 4) * 8 + (sy // 2) * 4 + lax.rem(d, 4))
            else:
                q, step, tt, ss = ((d // 8) * 16 + lax.rem(d, 8), 8, core + 2 * (d // 8), lax.rem(d, 8) * 4 + sz)
            rows = [t1[pl.ds(q + e * step, 16, stride=32), :] for e in range(2)]
            a2[m, d] = jnp.concatenate(rows, axis=0).astype(BF16)

            @pl.when(j > 0)
            def _():
                remote(a2.at[m, d], r2.at[m, w2[m]], asend.at[3 + m], arecv.at[3 + m], tt, ss).start()

            return carry

        lax.fori_loop(0, 16, share_a, 0)
        r2[m, w2[m]] = a2[m, w2[m]]

    for y in range(2):
        forward_cot(y).wait_recv()
    wait_bytes(pz.at[pl.ds(0, 15)], pr.at[0])

    @pl.when(jnp.logical_and(group > 0, z > 0))
    def _():
        wait_bytes(edges.at[0], pr.at[1])

    @pl.when(jnp.logical_and(group < SPACE - ZG, z < ZG - 1))
    def _():
        wait_bytes(edges.at[1], pr.at[2])

    for f in range(4):
        x = edges[0, f].astype(F32)
        pz[f] = jnp.concatenate([pltpu.roll(x, 64, 1), x], axis=0).astype(BF16)
        x = edges[1, f].astype(F32)
        pz[20 + f] = jnp.concatenate([x, pltpu.roll(x, 64, 1)], axis=0).astype(BF16)

    def spread(k, carry):
        block, f = (k // 4, lax.rem(k, 4))
        own = pz[(block + 1) * 4 + f].astype(F32)
        before = pltpu.roll(pz[block * 4 + f].astype(F32), 64, 1)
        after = pltpu.roll(pz[(block + 2) * 4 + f].astype(F32), 64, 1)
        turned = pltpu.roll(own, 64, 1)
        rows = [jnp.where(low, before, turned), own, jnp.where(low, turned, after)]
        for b in range(3):
            x = rows[b]
            cols = [jnp.where(first, 0.0, pltpu.roll(x, 1, 1)), x, jnp.where(last, 0.0, pltpu.roll(x, 127, 1))]
            for c in range(3):
                zz[block, 1 + f, pl.ds((b * 3 + c) * 64, 64), :] = cols[c].astype(BF16)
        return carry

    lax.fori_loop(0, 16, spread, 0)
    for a in range(3):
        lhs = jnp.concatenate([zz[block, f + a] for block in range(4) for f in range(4)], axis=1)
        outb[pl.ds(a * 576, 576), :] = dot(lhs, cw[...].reshape(2048, 128))

    def share_b(j, carry):
        ss = lax.rem(s + j, SPACE)
        o = 2 * ss
        piece = jnp.concatenate([outb[pl.ds(o, 32, stride=64), :], outb[pl.ds(o + 1, 32, stride=64), :]], axis=0)
        sb[ss] = piece.astype(BF16)

        @pl.when(j > 0)
        def _():
            remote(sb.at[ss], rb.at[s], bs, br, t, ss).start()

        return carry

    lax.fori_loop(0, SPACE, share_b, 0)
    rb[s] = sb[s]

    for m in range(3):
        second(m)

    halo_wait(gs.at[1], gs.at[1], 1, (0, 1), gsend, grecv)
    corners(gs.at[1], gsend, grecv, "recv")
    fill_shifts(gs, False)
    for f in range(2):
        parts = [gs[2 - c, f + 2 - a, pl.ds(2 - b, 4)].reshape(512, 256) for a, b, c in TAPS]
        total = dot(jnp.concatenate(parts, axis=1), wt[...])
        gf_out[f] = total.reshape(4, 128, 128).astype(BF16)

    wait_bytes(rb.at[pl.ds(0, 31)], br)
    for k in range(4):
        def add_b(g, total, k=k):
            return total + rb[g * 4 + k].astype(F32)

        fin[...] = lax.fori_loop(0, 8, add_b, jnp.zeros((64, 128), F32))
        for n, (a, b, c) in enumerate(TAPS):
            gb_out[a, b, c, :, pl.ds(k * 128, 128)] = fin[pl.ds(n, 2, stride=32), :]
    for m in range(3):
        wait_bytes(r2.at[m, pl.ds(0, 15)], arecv.at[3 + m])

        def add_a(k, total, m=m):
            return total + r2[m, k].astype(F32)

        fin[pl.ds(0, 32), :] = lax.fori_loop(0, 16, add_a, jnp.zeros((32, 128), F32))
        for b in range(3):
            for c in range(3):
                ga_out[m, b, c] = fin[pl.ds(b * 3 + c, 2, stride=16), :]

    for d in range(4):
        @pl.when(valid(t, s, *SIDES[d]))
        def _(d=d):
            halo_copy(feat, xs.at[1], 0, d, fs, fr).wait_send()
            halo_copy(gs.at[1], gs.at[1], 1, d, gsend, grecv).wait_send()
    corners(xs.at[1], fs, fr, "send")
    corners(gs.at[1], gsend, grecv, "send")
    for ds in (-1, 1):
        @pl.when(valid(t, s, 0, ds))
        def _(ds=ds):
            cot_row(ds).wait_send()
    for dt in (-1, 1):
        for ds in (-1, 0, 1):
            @pl.when(valid(t, s, dt, ds))
            def _(dt=dt, ds=ds):
                cot_col(dt, ds).wait_send()
    wait_bytes(cw.at[0, :, :, pl.ds(0, 16), :], ws.at[0])
    wait_bytes(cw.at[pl.ds(0, 3), :, :, pl.ds(0, 32), :], ws.at[1])
    for y in range(2):
        forward_cot(y).wait_send()
    for k in range(1, TM):
        give_tile(k).wait_send()
    wait_bytes(pz.at[pl.ds(0, 15)], ps.at[0])

    @pl.when(jnp.logical_and(z == 0, s > 0))
    def _():
        wait_bytes(edges.at[0], ps.at[1])
        wait_bytes(pz.at[pl.ds(0, 6)], ps.at[3])

    @pl.when(jnp.logical_and(z == ZG - 1, s < SPACE - 1))
    def _():
        wait_bytes(edges.at[0], ps.at[2])
        wait_bytes(pz.at[pl.ds(0, 6)], ps.at[4])

    for m in range(3):
        give_pair(m).wait_send()
        wait_bytes(r1.at[m, pl.ds(0, 3)], asend.at[m])
        wait_bytes(r2.at[m, pl.ds(0, 15)], asend.at[3 + m])
    wait_bytes(rb.at[pl.ds(0, 31)], bs)


def shards(features, weight_a, weight_b, cotangent):
    vmem = pl.BlockSpec(memory_space=pltpu.VMEM)
    far = pl.BlockSpec(memory_space=pl.ANY)
    dma = pltpu.SemaphoreType.DMA
    gf, ga, gb = pl.pallas_call(
        body,
        out_shape=(
            jax.ShapeDtypeStruct((2, 4, 128, 128), BF16),
            jax.ShapeDtypeStruct((3, 3, 3, 2, 128), F32),
            jax.ShapeDtypeStruct((3, 3, 3, 2, 512), F32),
        ),
        in_specs=[far, far, far, far],
        out_specs=(vmem, vmem, vmem),
        scratch_shapes=[
            pltpu.VMEM((3456, 256), BF16),
            pltpu.VMEM((27, 256, 512), BF16),
            pltpu.VMEM((3, 4, 6, 128, 128), BF16),
            pltpu.VMEM((3, 6, 4, 16, 512), BF16),
            pltpu.VMEM((4, 4, 2, 64, 128), BF16),
            pltpu.VMEM((2, 16, 512), BF16),
            pltpu.VMEM((2, 3, 16, 512), BF16),
            pltpu.VMEM((2, 3, 16, 512), F32),
            pltpu.VMEM((4, 2, 16, 256), BF16),
            pltpu.VMEM((2, 64, 256), BF16),
            pltpu.VMEM((1024, 256), F32),
            pltpu.VMEM((2, 128, 128), F32),
            pltpu.VMEM((4, 64, 128), BF16),
            pltpu.VMEM((24, 64, 128), BF16),
            pltpu.VMEM((3, 4, 6, 128, 256), BF16),
            pltpu.VMEM((256, 1024), BF16),
            pltpu.VMEM((4, 6, 576, 128), BF16),
            pltpu.VMEM((6912, 128), F32),
            pltpu.VMEM((2048, 128), F32),
            pltpu.VMEM((32, 64, 128), BF16),
            pltpu.VMEM((32, 64, 128), BF16),
            pltpu.VMEM((27, 2, 64, 128), BF16),
            pltpu.VMEM((27, 2, 64, 128), BF16),
            pltpu.VMEM((2, 64, 128), F32),
            pltpu.VMEM((3, 4, 288, 128), BF16),
            pltpu.VMEM((3, 4, 288, 128), BF16),
            pltpu.VMEM((512, 128), F32),
            pltpu.VMEM((3, 16, 32, 128), BF16),
            pltpu.VMEM((3, 16, 32, 128), BF16),
            pltpu.VMEM((2, 16, 512), F32),
            pltpu.VMEM((2, 128, 128), F32),
            pltpu.VMEM((2, 4, 32, 128), BF16),
            pltpu.VMEM((2, 4, 32, 128), BF16),
            pltpu.VMEM((64, 128), F32),
            pltpu.VMEM((4608, 128), BF16),
            pltpu.VMEM((3, 256, 128), F32),
            pltpu.VMEM((6912, 128), BF16),
            dma((5,)), dma((8,)), dma((8,)), dma((8,)), dma((8,)), dma((4,)), dma((4,)),
            dma((3,)), dma((3,)), dma((5,)), dma((3,)), dma((8,)), dma((8,)),
            dma, dma, dma((3,)), dma((3,)), dma((6,)), dma((6,)),
        ],
        compiler_params=pltpu.CompilerParams(collective_id=0, has_side_effects=True, vmem_limit_bytes=56 * 2**20),
    )(features, weight_a.reshape(3456, 256), weight_b.reshape(27, 256, 512), cotangent)
    return (gf, ga.transpose(0, 1, 2, 4, 3), gb)


def solution(mesh):
    placed = (P("tm", "space", None, None), P(), P(), P(None, "space", "tm", None))
    return jax.shard_map(
        shards,
        mesh=mesh,
        in_specs=placed,
        out_specs=(
            P("tm", "space", None, None),
            P(None, None, None, None, ("tm", "space")),
            P(None, None, None, ("tm", "space"), None),
        ),
        check_vma=False,
    )
```

```python
import jax
import jax.numpy as jnp
from jax import lax
from jax.experimental import pallas as pl
from jax.experimental.pallas import tpu as pltpu
from jax.sharding import PartitionSpec as P

F32 = jnp.float32
BF16 = jnp.bfloat16
MESH = pl.DeviceIdType.MESH
TM = 4
SPACE = 32
ZG = 4
SIDES = [(-1, 0), (1, 0), (0, -1), (0, 1)]
CORNERS = [(dt, ds) for dt in (-1, 1) for ds in (-1, 1)]
TAPS = [(a, b, c) for a in range(3) for b in range(3) for c in range(3)]
NT = (((1,), (1,)), ((), ()))


def dot(a, b):
    return lax.dot_general(a, b, (((1,), (0,)), ((), ())), preferred_element_type=F32)


def dot_nt(a, b):
    return lax.dot_general(a, b, NT, preferred_element_type=F32)


def valid(t, s, dt, ds):
    ok = jnp.bool_(True)
    if dt == 1:
        ok = t < TM - 1
    if dt == -1:
        ok = t > 0
    if ds == 1:
        ok = jnp.logical_and(ok, s < SPACE - 1)
    if ds == -1:
        ok = jnp.logical_and(ok, s > 0)
    return ok


def source_span(d, size):
    return (0, size) if d == 0 else ((size - 1, 1) if d == 1 else (0, 1))


def landing_span(d, size):
    return (1, size) if d == 0 else ((0, 1) if d == 1 else (size + 1, 1))


def shift_rows(x, step):
    rows = x.shape[0]
    index = lax.broadcasted_iota(jnp.int32, x.shape, 0)
    if step == 1:
        return jnp.where(index == 0, 0.0, pltpu.roll(x, 1, 0))
    return jnp.where(index == rows - 1, 0.0, pltpu.roll(x, rows - 1, 0))


def fill_edges(buf, t, s):
    @pl.when(t == 0)
    def _():
        buf[1, 0] = jnp.zeros(buf.shape[2:], BF16)

    @pl.when(t == TM - 1)
    def _():
        buf[1, 3] = jnp.zeros(buf.shape[2:], BF16)

    @pl.when(s == 0)
    def _():
        for f in range(4):
            buf[1, f, 0] = jnp.zeros(buf.shape[3:], BF16)

    @pl.when(s == SPACE - 1)
    def _():
        for f in range(4):
            buf[1, f, 5] = jnp.zeros(buf.shape[3:], BF16)


def fill_shifts(buf, own):
    def shift(f, r):
        x = buf[1, f, r].astype(F32)
        buf[0, f, r] = shift_rows(x, 1).astype(BF16)
        buf[2, f, r] = shift_rows(x, -1).astype(BF16)

    def inner(k, carry):
        shift(1 + k // 4, 1 + lax.rem(k, 4))
        return carry

    def frames(k, carry):
        shift(3 * (k // 6), lax.rem(k, 6))
        return carry

    def rows(k, carry):
        shift(1 + k // 2, 5 * lax.rem(k, 2))
        return carry

    if own:
        lax.fori_loop(0, 8, inner, 0)
    else:
        lax.fori_loop(0, 12, frames, 0)
        lax.fori_loop(0, 4, rows, 0)


def body(
    feat, wa_hbm, wb_hbm, cot,
    gf_out, ga_out, gb_out,
    wa, wb, xs, cs, cw, col, colh, colf, gps, gpl, pre, pool, pt, pz, gs, gt, zz, outa, outb,
    sb, rb, pxs, pxr, su, a1, r1, t1, a2, r2, tmp, pld, edge, edges, fin, ct, ya, wt,
    wsem, fs, fr, hs, hr, ws, wr, qs, qr, ps, pr, gsend, grecv, bs, br, xsend, xrecv, asend, arecv,
):
    t = lax.axis_index("tm")
    s = lax.axis_index("space")
    z = lax.rem(s, ZG)
    group = s - z
    core = lax.rem(t, 2)
    pair = t // 2

    def remote(src, dst, send, recv, tt, ss):
        return pltpu.make_async_remote_copy(
            src_ref=src, dst_ref=dst, send_sem=send, recv_sem=recv, device_id=(tt, ss), device_id_type=MESH
        )

    def wait_bytes(ref, sem):
        pltpu.make_async_copy(ref, ref, sem).wait()

    load_wa = pltpu.make_async_copy(wa_hbm, wa, wsem.at[0])
    load_wb = pltpu.make_async_copy(wb_hbm, wb, wsem.at[1])
    keep_tile = pltpu.make_async_copy(cot, cs.at[1, pl.ds(1, 4), pl.ds(1, 2)], wsem.at[3])
    keep_feat = pltpu.make_async_copy(feat, xs.at[1, pl.ds(1, 2), pl.ds(1, 4)], wsem.at[4])
    keep_tile.start()
    keep_feat.start()
    load_wa.start()
    load_wb.start()

    barrier = pltpu.get_barrier_semaphore()

    def greet(tt, ss):
        pl.semaphore_signal(barrier, inc=1, device_id=(tt, ss), device_id_type=MESH)

    def greet_near(j, carry):
        ss = group - ZG + lax.rem(j, 12)

        @pl.when(jnp.logical_and(ss >= 0, ss < SPACE))
        def _():
            greet(1 - core + 2 * (j // 12), ss)

        return carry

    def greet_far(j, carry):
        @pl.when(j > 0)
        def _():
            greet(core + 2 * lax.rem(pair + j // 32, 2), lax.rem(s + j, SPACE))

        return carry

    lax.fori_loop(0, 24, greet_near, 0)
    lax.fori_loop(0, 64, greet_far, 0)
    greeted = 63 + 24 - jnp.where(group == 0, 8, 0) - jnp.where(group == SPACE - ZG, 8, 0)

    pl.semaphore_wait(barrier, greeted)

    lane_id = lax.broadcasted_iota(jnp.int32, (64, 128), 1)
    low = lane_id < 64
    first = lax.rem(lane_id, 64) == 0
    last = lax.rem(lane_id, 64) == 63

    def halo_copy(source, target, base, d, send, recv):
        dt, ds = SIDES[d]
        f0, fn = source_span(dt, 2)
        r0, rn = source_span(ds, 4)
        lf, _ = landing_span(dt, 2)
        lr, _ = landing_span(ds, 4)
        return remote(
            source.at[pl.ds(base + f0, fn), pl.ds(base + r0, rn)],
            target.at[pl.ds(lf, fn), pl.ds(lr, rn)],
            send.at[d], recv.at[d], t + dt, s + ds,
        )

    def halo_wait(source, target, base, ways, send, recv):
        for d in ways:
            dt, ds = SIDES[d]

            @pl.when(valid(t, s, -dt, -ds))
            def _(d=d):
                halo_copy(source, target, base, d, send, recv).wait_recv()

    def corner_copy(target, d, send, recv):
        dt, ds = CORNERS[d]
        row = pl.ds(0 if ds == 1 else 5, 1)
        return remote(
            target.at[pl.ds(2 if dt == 1 else 1, 1), row],
            target.at[pl.ds(0 if dt == 1 else 3, 1), row],
            send.at[4 + d], recv.at[4 + d], t + dt, s,
        )

    def corner_valid(d, arriving):
        dt, ds = CORNERS[d]
        return jnp.logical_and(valid(t, s, -dt if arriving else dt, 0), valid(t, s, 0, -ds))

    def corners(target, send, recv, what):
        for d in range(4):
            @pl.when(corner_valid(d, what == "recv"))
            def _(d=d):
                copy = corner_copy(target, d, send, recv)
                if what == "start":
                    copy.start()
                elif what == "recv":
                    copy.wait_recv()
                else:
                    copy.wait_send()

    for d in range(4):
        @pl.when(valid(t, s, *SIDES[d]))
        def _(d=d):
            halo_copy(feat, xs.at[1], 0, d, fs, fr).start()

    def cot_row(ds):
        r0, _ = source_span(ds, 2)
        lr, _ = landing_span(ds, 2)
        k = 0 if ds == -1 else 1
        return remote(
            cot.at[:, pl.ds(r0, 1)], cs.at[1, pl.ds(1, 4), pl.ds(lr, 1)], hs.at[k], hr.at[k], t, s + ds
        )

    for ds in (-1, 1):
        @pl.when(valid(t, s, 0, ds))
        def _(ds=ds):
            cot_row(ds).start()

    keep_tile.wait()
    tmp[...] = jnp.zeros_like(tmp)
    for f in range(4):
        for r in range(2):
            x = cs[1, 1 + f, 1 + r].astype(F32)
            k = f * 2 + r
            tmp[0, pl.ds(k, 1), :] = x[0:1, :]
            tmp[1, pl.ds(k, 1), :] = x[15:16, :]
    col[...] = tmp[...].astype(BF16)

    def cot_col(dt, ds):
        side = 0 if dt == 1 else 1
        k = 2 + side * 3 + ds + 1
        return remote(
            col.at[1 if dt == 1 else 0], colh.at[side, 1 - ds], hs.at[k], hr.at[k], t + dt, s + ds
        )

    for dt in (-1, 1):
        for ds in (-1, 0, 1):
            @pl.when(valid(t, s, dt, ds))
            def _(dt=dt, ds=ds):
                cot_col(dt, ds).start()

    def gather_cot(j, tt, zd):
        return remote(
            cot.at[:, :, :, pl.ds(pl.multiple_of(zd * 128, 128), 128)],
            cw.at[z, :, :, pl.ds(pl.multiple_of(t * 16, 16), 16), :],
            ws.at[0 if j == 4 else 1], wr.at[0 if j == 4 else 1], tt, group + zd,
        )

    for j in range(1, 8):
        gather_cot(j, core + 2 * lax.rem(pair + j // 4, 2), lax.rem(z + j % 4, ZG)).start()
    keep_cot = pltpu.make_async_copy(
        cot.at[:, :, :, pl.ds(pl.multiple_of(z * 128, 128), 128)],
        cw.at[z, :, :, pl.ds(pl.multiple_of(t * 16, 16), 16), :],
        wsem.at[2],
    )
    keep_cot.start()

    fill_edges(xs, t, s)
    fill_edges(gs, t, s)
    @pl.when(t == 0)
    def _():
        colh[0] = jnp.zeros(colh.shape[1:], BF16)

    @pl.when(t == TM - 1)
    def _():
        colh[1] = jnp.zeros(colh.shape[1:], BF16)

    @pl.when(s == 0)
    def _():
        for side in range(2):
            colh[side, 0] = jnp.zeros(colh.shape[2:], BF16)
        for f in range(4):
            cs[1, 1 + f, 0] = jnp.zeros(cs.shape[3:], BF16)

    @pl.when(s == SPACE - 1)
    def _():
        for side in range(2):
            colh[side, 2] = jnp.zeros(colh.shape[2:], BF16)
        for f in range(4):
            cs[1, 1 + f, 3] = jnp.zeros(cs.shape[3:], BF16)

    @pl.when(group == SPACE - ZG)
    def _():
        edges[1] = jnp.zeros(edges.shape[1:], BF16)

    @pl.when(group == 0)
    def _():
        edges[0] = jnp.zeros(edges.shape[1:], BF16)

    t1[...] = jnp.zeros_like(t1)
    for k in range(27, 32):
        outb[pl.ds(k * 64, 64), :] = jnp.zeros((64, 128), F32)
    for k in range(4):
        zz[k, 0] = jnp.zeros(zz.shape[2:], BF16)
        zz[k, 5] = jnp.zeros(zz.shape[2:], BF16)

    load_wa.wait()
    for n in range(27):
        wt[pl.ds(n * 256, 256), :] = wa[pl.ds(n * 128, 128), :].astype(F32).T.astype(BF16)
    keep_feat.wait()
    fill_shifts(xs, True)
    for ds in (-1, 1):
        @pl.when(valid(t, s, 0, -ds))
        def _(ds=ds):
            cot_row(ds).wait_recv()
    for dt in (-1, 1):
        for ds in (-1, 0, 1):
            @pl.when(valid(t, s, -dt, -ds))
            def _(dt=dt, ds=ds):
                cot_col(dt, ds).wait_recv()
    halo_wait(feat, xs.at[1], 0, (2, 3), fs, fr)
    corners(xs.at[1], fs, fr, "start")
    colf[...] = colh[...].astype(F32)
    index = lax.broadcasted_iota(jnp.int32, (16, 512), 0)
    for f in range(4):
        for r in range(4):
            j = (0, 1, 1, 2)[r]
            k = f * 2 + (1, 0, 1, 0)[r]
            x = cs[1, 1 + f, r].astype(F32)
            left = colf[0, j, pl.ds(k, 1), :]
            right = colf[1, j, pl.ds(k, 1), :]
            cs[0, 1 + f, r] = jnp.where(index == 0, left, pltpu.roll(x, 1, 0)).astype(BF16)
            cs[2, 1 + f, r] = jnp.where(index == 15, right, pltpu.roll(x, 15, 0)).astype(BF16)
    load_wb.wait()
    for b in range(3):
        for c in range(3):
            tile = cs[2 - c, pl.ds(1, 4), pl.ds(2 - b, 2)].reshape(128, 512)
            ct[pl.ds((b * 3 + c) * 512, 512), :] = tile.astype(F32).T.astype(BF16)
    for a in range(3):
        ya[a] = dot(jnp.concatenate([wb[a * 9 + n] for n in range(9)], axis=1), ct[...])
    cell = lax.broadcasted_iota(jnp.int32, (256, 128), 1)
    later = jnp.where(cell < 96, pltpu.roll(ya[0], 96, 1), 0.0)
    earlier = jnp.where(cell >= 32, pltpu.roll(ya[2], 32, 1), 0.0)
    gps[...] = (ya[1] + later + earlier).T.reshape(4, 2, 16, 256).astype(BF16)

    partner = t + 1 - 2 * core

    def forward_cot(y):
        part = cw.at[:, :, :, pl.ds(pl.multiple_of((core + 2 * y) * 16, 16), 16), :]
        return remote(part, part, ws.at[2 + y], wr.at[2 + y], partner, s)

    def give_tile(k):
        tt = lax.rem(t + k, TM)
        return remote(
            gps.at[tt], gpl.at[:, pl.ds(pl.multiple_of(t * 16, 16), 16), :], qs.at[k - 1], qr.at[k - 1], tt, s
        )

    for k in range(1, TM):
        give_tile(k).start()
    gpl[:, pl.ds(pl.multiple_of(t * 16, 16), 16), :] = gps[t]
    wait_bytes(cw.at[0, :, :, pl.ds(0, 16), :], wr.at[0])
    wait_bytes(cw.at[pl.ds(0, 3), :, :, pl.ds(0, 32), :], wr.at[1])
    keep_cot.wait()
    for y in range(2):
        forward_cot(y).start()

    halo_wait(feat, xs.at[1], 0, (0, 1), fs, fr)
    corners(xs.at[1], fs, fr, "recv")
    fill_shifts(xs, False)
    for f in range(2):
        parts = [xs[c, f + a, pl.ds(b, 4)].reshape(512, 128) for a, b, c in TAPS]
        pre[pl.ds(f * 512, 512), :] = dot(jnp.concatenate(parts, axis=1), wa[...])
    for q in range(2):
        summed = jnp.zeros((128, 256), F32)
        for f in range(2):
            for r in range(2):
                rows = pl.ds((f * 4 + q * 2 + r) * 128, 128)
                p = pre[rows, :]
                sig = jax.nn.sigmoid(p)
                summed = summed + p * sig
                pre[rows, :] = sig * (1.0 + p * (1.0 - sig))
        for lane in range(2):
            pool[lane] = summed[:, lane * 128 : lane * 128 + 128]
        for lane in range(2):
            even = pool[lane, pl.ds(0, 64, stride=2), :]
            odd = pool[lane, pl.ds(1, 64, stride=2), :]
            pld[lane, pl.ds(q * 64, 64), :] = (even + odd) * 0.125
    for lane in range(2):
        turned = pld[lane].astype(BF16).astype(F32).T
        for half in range(2):
            block = turned[half * 64 : half * 64 + 64]
            pt[2 * lane + half] = block.astype(BF16)
            top, bottom = (block[0:32], block[32:64])
            edge[0, 2 * lane + half] = jnp.where(low[0:32], top, pltpu.roll(bottom, 64, 1)).astype(BF16)
            edge[1, 2 * lane + half] = jnp.where(low[0:32], pltpu.roll(top, 64, 1), bottom).astype(BF16)

    def give_pooled(tt, ss):
        return remote(pt.at[tt], pz.at[(z + 1) * 4 + t], ps.at[0], pr.at[0], tt, ss)

    def give_edge(tt, ss, k):
        return remote(edge.at[k, tt], edges.at[1 - k, t], ps.at[1 + k], pr.at[2 - k], tt, ss)

    for j in range(1, 16):
        give_pooled(lax.rem(t + j // 4, TM), group + lax.rem(z + j % 4, ZG)).start()
    pz[(z + 1) * 4 + t] = pt[t]

    for k, inside, ss in ((0, jnp.logical_and(z == 0, s > 0), s - 1), (1, jnp.logical_and(z == ZG - 1, s < SPACE - 1), s + 1)):
        @pl.when(inside)
        def _(k=k, ss=ss):
            for j in range(1, TM):
                give_edge(lax.rem(t + j, TM), ss, k).start()
            give_edge(t, ss, k).start()

    for k in range(1, TM):
        give_tile(k).wait_recv()
    for q in range(2):
        u = gpl[q].astype(F32) * 0.125
        for lane in range(2):
            half = u[:, lane * 128 : lane * 128 + 128]
            pool[lane, pl.ds(0, 64, stride=2), :] = half
            pool[lane, pl.ds(1, 64, stride=2), :] = half
        for f in range(2):
            for r in range(2):
                k = f * 4 + q * 2 + r
                for lane in range(2):
                    g = pool[lane] * pre[pl.ds(k * 128, 128), pl.ds(lane * 128, 128)]
                    gs[1, 1 + f, 1 + q * 2 + r, :, pl.ds(lane * 128, 128)] = g.astype(BF16)
                    gt[pl.ds(lane * 128, 128), pl.ds(k * 128, 128)] = g.T.astype(BF16)
    for d in range(4):
        @pl.when(valid(t, s, *SIDES[d]))
        def _(d=d):
            halo_copy(gs.at[1], gs.at[1], 1, d, gsend, grecv).start()

    def pass_edge(k, zd):
        return remote(edges.at[k], edges.at[k], ps.at[3 + k], pr.at[1 + k], t, group + zd)

    for k, passes in ((0, jnp.logical_and(z == 0, s > 0)), (1, jnp.logical_and(z == ZG - 1, s < SPACE - 1))):
        @pl.when(passes)
        def _(k=k):
            wait_bytes(edges.at[k], pr.at[1 + k])
            for j in range(1, ZG):
                pass_edge(k, lax.rem(z + j, ZG)).start()


    def give_pair(m):
        taps = pl.ds(m * 9, 9)
        return remote(pxs.at[taps], pxr.at[taps], xsend.at[m], xrecv.at[m], partner, s)

    for m in range(3):
        rhs = [xs[c, pl.ds(m, 2), pl.ds(b, 4)].reshape(1024, 128) for b in range(3) for c in range(3)]
        res = dot(gt[...], jnp.concatenate(rhs, axis=1))
        for k in range(9):
            outa[pl.ds((m * 9 + k) * 256, 256), :] = res[:, k * 128 : k * 128 + 128]

        def cut_a(k, carry, m=m):
            n = m * 9 + k
            for y in range(2):
                other = pl.multiple_of(n * 256 + (1 - core + 2 * y) * 64, 64)
                pxs[n, y] = outa[pl.ds(other, 64), :].astype(BF16)
            return carry

        lax.fori_loop(0, 9, cut_a, 0)
        give_pair(m).start()
    halo_wait(gs.at[1], gs.at[1], 1, (2, 3), gsend, grecv)
    corners(gs.at[1], gsend, grecv, "start")
    fill_shifts(gs, True)

    sx, sy, sz = (s // 8, 2 * lax.rem(s // 4, 2) + pair, z)

    def place(x, y, zed):
        return (core + 2 * lax.rem(y, 2), x * 8 + (y // 2) * 4 + zed)

    coord = (sx, sy, sz)
    for m in range(3):
        give_pair(m).wait_recv()

        def add_pair(i, carry, m=m):
            n = m * 9 + i
            for y in range(2):
                own = pl.multiple_of(n * 256 + (core + 2 * y) * 64, 64)
                su[y] = outa[pl.ds(own, 64), :] + pxr[n, y].astype(F32)
            for v in range(4):
                if m == 0:
                    rows = [su[y, pl.ds(v * 16, 16), :] for y in range(2)]
                elif m == 1:
                    rows = [su[v % 2, pl.ds(x * 16 + (v // 2) * 8, 8), :] for x in range(4)]
                else:
                    rows = [su[y, pl.ds(v * 2 + e, 8, stride=8), :] for y in range(2) for e in range(2)]
                at = pl.ds(pl.multiple_of(i * 32, 32), 32)
                a1[m, v, at, :] = jnp.concatenate(rows, axis=0).astype(BF16)
            return carry

        lax.fori_loop(0, 9, add_pair, 0)
        for k in range(1, 4):
            v = lax.rem(coord[m] + k, 4)
            to = [sx, sy, sz]
            to[m] = v
            remote(a1.at[m, v], r1.at[m, coord[m]], asend.at[m], arecv.at[m], *place(*to)).start()
        r1[m, coord[m]] = a1[m, coord[m]]

    w2 = (pair * 8 + lax.rem(s, 8), sx * 4 + sz, pair * 8 + s // 4)

    def second(m):
        wait_bytes(r1.at[m, pl.ds(0, 3)], arecv.at[m])
        total = r1[m, 0].astype(F32)
        for k in range(1, 4):
            total = total + r1[m, k].astype(F32)
        t1[pl.ds(0, 288), :] = total

        def share_a(j, carry):
            d = lax.rem(w2[m] + j, 16)
            if m == 0:
                q, step, tt, ss = (d * 2, 1, core + 2 * (d // 8), sx * 8 + lax.rem(d, 8))
            elif m == 1:
                q, step, tt, ss = (d * 2, 1, t, (d // 4) * 8 + (sy // 2) * 4 + lax.rem(d, 4))
            else:
                q, step, tt, ss = ((d // 8) * 16 + lax.rem(d, 8), 8, core + 2 * (d // 8), lax.rem(d, 8) * 4 + sz)
            rows = [t1[pl.ds(q + e * step, 16, stride=32), :] for e in range(2)]
            a2[m, d] = jnp.concatenate(rows, axis=0).astype(BF16)

            @pl.when(j > 0)
            def _():
                remote(a2.at[m, d], r2.at[m, w2[m]], asend.at[3 + m], arecv.at[3 + m], tt, ss).start()

            return carry

        lax.fori_loop(0, 16, share_a, 0)
        r2[m, w2[m]] = a2[m, w2[m]]

    for y in range(2):
        forward_cot(y).wait_recv()
    wait_bytes(pz.at[pl.ds(0, 15)], pr.at[0])

    @pl.when(jnp.logical_and(group > 0, z > 0))
    def _():
        wait_bytes(edges.at[0], pr.at[1])

    @pl.when(jnp.logical_and(group < SPACE - ZG, z < ZG - 1))
    def _():
        wait_bytes(edges.at[1], pr.at[2])

    for f in range(4):
        x = edges[0, f].astype(F32)
        pz[f] = jnp.concatenate([pltpu.roll(x, 64, 1), x], axis=0).astype(BF16)
        x = edges[1, f].astype(F32)
        pz[20 + f] = jnp.concatenate([x, pltpu.roll(x, 64, 1)], axis=0).astype(BF16)

    def spread(k, carry):
        block, f = (k // 4, lax.rem(k, 4))
        own = pz[(block + 1) * 4 + f].astype(F32)
        before = pltpu.roll(pz[block * 4 + f].astype(F32), 64, 1)
        after = pltpu.roll(pz[(block + 2) * 4 + f].astype(F32), 64, 1)
        turned = pltpu.roll(own, 64, 1)
        rows = [jnp.where(low, before, turned), own, jnp.where(low, turned, after)]
        for b in range(3):
            x = rows[b]
            cols = [jnp.where(first, 0.0, pltpu.roll(x, 1, 1)), x, jnp.where(last, 0.0, pltpu.roll(x, 127, 1))]
            for c in range(3):
                zz[block, 1 + f, pl.ds((b * 3 + c) * 64, 64), :] = cols[c].astype(BF16)
        return carry

    lax.fori_loop(0, 16, spread, 0)
    for a in range(3):
        lhs = jnp.concatenate([zz[block, f + a] for block in range(4) for f in range(4)], axis=1)
        outb[pl.ds(a * 576, 576), :] = dot(lhs, cw[...].reshape(2048, 128))

    def share_b(j, carry):
        ss = lax.rem(s + j, SPACE)
        o = 2 * ss
        piece = jnp.concatenate([outb[pl.ds(o, 32, stride=64), :], outb[pl.ds(o + 1, 32, stride=64), :]], axis=0)
        sb[ss] = piece.astype(BF16)

        @pl.when(j > 0)
        def _():
            remote(sb.at[ss], rb.at[s], bs, br, t, ss).start()

        return carry

    lax.fori_loop(0, SPACE, share_b, 0)
    rb[s] = sb[s]

    for m in range(3):
        second(m)

    halo_wait(gs.at[1], gs.at[1], 1, (0, 1), gsend, grecv)
    corners(gs.at[1], gsend, grecv, "recv")
    fill_shifts(gs, False)
    for f in range(2):
        parts = [gs[2 - c, f + 2 - a, pl.ds(2 - b, 4)].reshape(512, 256) for a, b, c in TAPS]
        total = dot(jnp.concatenate(parts, axis=1), wt[...])
        gf_out[f] = total.reshape(4, 128, 128).astype(BF16)

    wait_bytes(rb.at[pl.ds(0, 31)], br)
    for k in range(4):
        def add_b(g, total, k=k):
            return total + rb[g * 4 + k].astype(F32)

        fin[...] = lax.fori_loop(0, 8, add_b, jnp.zeros((64, 128), F32))
        for n, (a, b, c) in enumerate(TAPS):
            gb_out[a, b, c, :, pl.ds(k * 128, 128)] = fin[pl.ds(n, 2, stride=32), :]
    for m in range(3):
        wait_bytes(r2.at[m, pl.ds(0, 15)], arecv.at[3 + m])

        def add_a(k, total, m=m):
            return total + r2[m, k].astype(F32)

        fin[pl.ds(0, 32), :] = lax.fori_loop(0, 16, add_a, jnp.zeros((32, 128), F32))
        for b in range(3):
            for c in range(3):
                ga_out[m, b, c] = fin[pl.ds(b * 3 + c, 2, stride=16), :]

    for d in range(4):
        @pl.when(valid(t, s, *SIDES[d]))
        def _(d=d):
            halo_copy(feat, xs.at[1], 0, d, fs, fr).wait_send()
            halo_copy(gs.at[1], gs.at[1], 1, d, gsend, grecv).wait_send()
    corners(xs.at[1], fs, fr, "send")
    corners(gs.at[1], gsend, grecv, "send")
    for ds in (-1, 1):
        @pl.when(valid(t, s, 0, ds))
        def _(ds=ds):
            cot_row(ds).wait_send()
    for dt in (-1, 1):
        for ds in (-1, 0, 1):
            @pl.when(valid(t, s, dt, ds))
            def _(dt=dt, ds=ds):
                cot_col(dt, ds).wait_send()
    wait_bytes(cw.at[0, :, :, pl.ds(0, 16), :], ws.at[0])
    wait_bytes(cw.at[pl.ds(0, 3), :, :, pl.ds(0, 32), :], ws.at[1])
    for y in range(2):
        forward_cot(y).wait_send()
    for k in range(1, TM):
        give_tile(k).wait_send()
    wait_bytes(pz.at[pl.ds(0, 15)], ps.at[0])

    @pl.when(jnp.logical_and(z == 0, s > 0))
    def _():
        wait_bytes(edges.at[0], ps.at[1])
        wait_bytes(pz.at[pl.ds(0, 6)], ps.at[3])

    @pl.when(jnp.logical_and(z == ZG - 1, s < SPACE - 1))
    def _():
        wait_bytes(edges.at[0], ps.at[2])
        wait_bytes(pz.at[pl.ds(0, 6)], ps.at[4])

    for m in range(3):
        give_pair(m).wait_send()
        wait_bytes(r1.at[m, pl.ds(0, 3)], asend.at[m])
        wait_bytes(r2.at[m, pl.ds(0, 15)], asend.at[3 + m])
    wait_bytes(rb.at[pl.ds(0, 31)], bs)


def shards(features, weight_a, weight_b, cotangent):
    vmem = pl.BlockSpec(memory_space=pltpu.VMEM)
    far = pl.BlockSpec(memory_space=pl.ANY)
    dma = pltpu.SemaphoreType.DMA
    gf, ga, gb = pl.pallas_call(
        body,
        out_shape=(
            jax.ShapeDtypeStruct((2, 4, 128, 128), BF16),
            jax.ShapeDtypeStruct((3, 3, 3, 2, 128), F32),
            jax.ShapeDtypeStruct((3, 3, 3, 2, 512), F32),
        ),
        in_specs=[far, far, far, far],
        out_specs=(vmem, vmem, vmem),
        scratch_shapes=[
            pltpu.VMEM((3456, 256), BF16),
            pltpu.VMEM((27, 256, 512), BF16),
            pltpu.VMEM((3, 4, 6, 128, 128), BF16),
            pltpu.VMEM((3, 6, 4, 16, 512), BF16),
            pltpu.VMEM((4, 4, 2, 64, 128), BF16),
            pltpu.VMEM((2, 16, 512), BF16),
            pltpu.VMEM((2, 3, 16, 512), BF16),
            pltpu.VMEM((2, 3, 16, 512), F32),
            pltpu.VMEM((4, 2, 16, 256), BF16),
            pltpu.VMEM((2, 64, 256), BF16),
            pltpu.VMEM((1024, 256), F32),
            pltpu.VMEM((2, 128, 128), F32),
            pltpu.VMEM((4, 64, 128), BF16),
            pltpu.VMEM((24, 64, 128), BF16),
            pltpu.VMEM((3, 4, 6, 128, 256), BF16),
            pltpu.VMEM((256, 1024), BF16),
            pltpu.VMEM((4, 6, 576, 128), BF16),
            pltpu.VMEM((6912, 128), F32),
            pltpu.VMEM((2048, 128), F32),
            pltpu.VMEM((32, 64, 128), BF16),
            pltpu.VMEM((32, 64, 128), BF16),
            pltpu.VMEM((27, 2, 64, 128), BF16),
            pltpu.VMEM((27, 2, 64, 128), BF16),
            pltpu.VMEM((2, 64, 128), F32),
            pltpu.VMEM((3, 4, 288, 128), BF16),
            pltpu.VMEM((3, 4, 288, 128), BF16),
            pltpu.VMEM((512, 128), F32),
            pltpu.VMEM((3, 16, 32, 128), BF16),
            pltpu.VMEM((3, 16, 32, 128), BF16),
            pltpu.VMEM((2, 16, 512), F32),
            pltpu.VMEM((2, 128, 128), F32),
            pltpu.VMEM((2, 4, 32, 128), BF16),
            pltpu.VMEM((2, 4, 32, 128), BF16),
            pltpu.VMEM((64, 128), F32),
            pltpu.VMEM((4608, 128), BF16),
            pltpu.VMEM((3, 256, 128), F32),
            pltpu.VMEM((6912, 128), BF16),
            dma((5,)), dma((8,)), dma((8,)), dma((8,)), dma((8,)), dma((4,)), dma((4,)),
            dma((3,)), dma((3,)), dma((5,)), dma((3,)), dma((8,)), dma((8,)),
            dma, dma, dma((3,)), dma((3,)), dma((6,)), dma((6,)),
        ],
        compiler_params=pltpu.CompilerParams(collective_id=0, has_side_effects=True, vmem_limit_bytes=56 * 2**20),
    )(features, weight_a.reshape(3456, 256), weight_b.reshape(27, 256, 512), cotangent)
    return (gf, ga.transpose(0, 1, 2, 4, 3), gb)


def solution(mesh):
    placed = (P("tm", "space", None, None), P(), P(), P(None, "space", "tm", None))
    return jax.shard_map(
        shards,
        mesh=mesh,
        in_specs=placed,
        out_specs=(
            P("tm", "space", None, None),
            P(None, None, None, None, ("tm", "space")),
            P(None, None, None, ("tm", "space"), None),
        ),
        check_vma=False,
    )
```

```python
import jax
import jax.numpy as jnp
from jax import lax
from jax.experimental import pallas as pl
from jax.experimental.pallas import tpu as pltpu
from jax.sharding import PartitionSpec as P

F32 = jnp.float32
BF16 = jnp.bfloat16
MESH = pl.DeviceIdType.MESH
TM = 4
SPACE = 32
ZG = 4
SIDES = [(-1, 0), (1, 0), (0, -1), (0, 1)]
CORNERS = [(dt, ds) for dt in (-1, 1) for ds in (-1, 1)]
TAPS = [(a, b, c) for a in range(3) for b in range(3) for c in range(3)]
NT = (((1,), (1,)), ((), ()))


def dot(a, b):
    return lax.dot_general(a, b, (((1,), (0,)), ((), ())), preferred_element_type=F32)


def dot_nt(a, b):
    return lax.dot_general(a, b, NT, preferred_element_type=F32)


def valid(t, s, dt, ds):
    ok = jnp.bool_(True)
    if dt == 1:
        ok = t < TM - 1
    if dt == -1:
        ok = t > 0
    if ds == 1:
        ok = jnp.logical_and(ok, s < SPACE - 1)
    if ds == -1:
        ok = jnp.logical_and(ok, s > 0)
    return ok


def source_span(d, size):
    return (0, size) if d == 0 else ((size - 1, 1) if d == 1 else (0, 1))


def landing_span(d, size):
    return (1, size) if d == 0 else ((0, 1) if d == 1 else (size + 1, 1))


def shift_rows(x, step):
    rows = x.shape[0]
    index = lax.broadcasted_iota(jnp.int32, x.shape, 0)
    if step == 1:
        return jnp.where(index == 0, 0.0, pltpu.roll(x, 1, 0))
    return jnp.where(index == rows - 1, 0.0, pltpu.roll(x, rows - 1, 0))


def fill_edges(buf, t, s):
    @pl.when(t == 0)
    def _():
        buf[1, 0] = jnp.zeros(buf.shape[2:], BF16)

    @pl.when(t == TM - 1)
    def _():
        buf[1, 3] = jnp.zeros(buf.shape[2:], BF16)

    @pl.when(s == 0)
    def _():
        for f in range(4):
            buf[1, f, 0] = jnp.zeros(buf.shape[3:], BF16)

    @pl.when(s == SPACE - 1)
    def _():
        for f in range(4):
            buf[1, f, 5] = jnp.zeros(buf.shape[3:], BF16)


def fill_shifts(buf, own):
    def shift(f, r):
        x = buf[1, f, r].astype(F32)
        buf[0, f, r] = shift_rows(x, 1).astype(BF16)
        buf[2, f, r] = shift_rows(x, -1).astype(BF16)

    def inner(k, carry):
        shift(1 + k // 4, 1 + lax.rem(k, 4))
        return carry

    def frames(k, carry):
        shift(3 * (k // 6), lax.rem(k, 6))
        return carry

    def rows(k, carry):
        shift(1 + k // 2, 5 * lax.rem(k, 2))
        return carry

    if own:
        lax.fori_loop(0, 8, inner, 0)
    else:
        lax.fori_loop(0, 12, frames, 0)
        lax.fori_loop(0, 4, rows, 0)


def body(
    feat, wa_hbm, wb_hbm, cot,
    gf_out, ga_out, gb_out,
    wa, wb, xs, cs, cw, col, colh, colf, gps, gpl, pre, pool, pt, pz, gs, gt, zz, outa, outb,
    sb, rb, pxs, pxr, su, a1, r1, t1, a2, r2, tmp, pld, edge, edges, fin, ct, ya, wt,
    wsem, fs, fr, hs, hr, ws, wr, qs, qr, ps, pr, gsend, grecv, bs, br, xsend, xrecv, asend, arecv,
):
    t = lax.axis_index("tm")
    s = lax.axis_index("space")
    z = lax.rem(s, ZG)
    group = s - z
    core = lax.rem(t, 2)
    pair = t // 2

    def remote(src, dst, send, recv, tt, ss):
        return pltpu.make_async_remote_copy(
            src_ref=src, dst_ref=dst, send_sem=send, recv_sem=recv, device_id=(tt, ss), device_id_type=MESH
        )

    def wait_bytes(ref, sem):
        pltpu.make_async_copy(ref, ref, sem).wait()

    load_wa = pltpu.make_async_copy(wa_hbm, wa, wsem.at[0])
    load_wb = pltpu.make_async_copy(wb_hbm, wb, wsem.at[1])
    keep_tile = pltpu.make_async_copy(cot, cs.at[1, pl.ds(1, 4), pl.ds(1, 2)], wsem.at[3])
    keep_feat = pltpu.make_async_copy(feat, xs.at[1, pl.ds(1, 2), pl.ds(1, 4)], wsem.at[4])
    keep_tile.start()
    keep_feat.start()
    load_wa.start()
    load_wb.start()

    barrier = pltpu.get_barrier_semaphore()

    def greet(tt, ss):
        pl.semaphore_signal(barrier, inc=1, device_id=(tt, ss), device_id_type=MESH)

    def greet_near(j, carry):
        ss = group - ZG + lax.rem(j, 12)

        @pl.when(jnp.logical_and(ss >= 0, ss < SPACE))
        def _():
            greet(1 - core + 2 * (j // 12), ss)

        return carry

    def greet_far(j, carry):
        @pl.when(j > 0)
        def _():
            greet(core + 2 * lax.rem(pair + j // 32, 2), lax.rem(s + j, SPACE))

        return carry

    lax.fori_loop(0, 24, greet_near, 0)
    lax.fori_loop(0, 64, greet_far, 0)
    greeted = 63 + 24 - jnp.where(group == 0, 8, 0) - jnp.where(group == SPACE - ZG, 8, 0)

    pl.semaphore_wait(barrier, greeted)

    lane_id = lax.broadcasted_iota(jnp.int32, (64, 128), 1)
    low = lane_id < 64
    first = lax.rem(lane_id, 64) == 0
    last = lax.rem(lane_id, 64) == 63

    def halo_copy(source, target, base, d, send, recv):
        dt, ds = SIDES[d]
        f0, fn = source_span(dt, 2)
        r0, rn = source_span(ds, 4)
        lf, _ = landing_span(dt, 2)
        lr, _ = landing_span(ds, 4)
        return remote(
            source.at[pl.ds(base + f0, fn), pl.ds(base + r0, rn)],
            target.at[pl.ds(lf, fn), pl.ds(lr, rn)],
            send.at[d], recv.at[d], t + dt, s + ds,
        )

    def halo_wait(source, target, base, ways, send, recv):
        for d in ways:
            dt, ds = SIDES[d]

            @pl.when(valid(t, s, -dt, -ds))
            def _(d=d):
                halo_copy(source, target, base, d, send, recv).wait_recv()

    def corner_copy(target, d, send, recv):
        dt, ds = CORNERS[d]
        row = pl.ds(0 if ds == 1 else 5, 1)
        return remote(
            target.at[pl.ds(2 if dt == 1 else 1, 1), row],
            target.at[pl.ds(0 if dt == 1 else 3, 1), row],
            send.at[4 + d], recv.at[4 + d], t + dt, s,
        )

    def corner_valid(d, arriving):
        dt, ds = CORNERS[d]
        return jnp.logical_and(valid(t, s, -dt if arriving else dt, 0), valid(t, s, 0, -ds))

    def corners(target, send, recv, what):
        for d in range(4):
            @pl.when(corner_valid(d, what == "recv"))
            def _(d=d):
                copy = corner_copy(target, d, send, recv)
                if what == "start":
                    copy.start()
                elif what == "recv":
                    copy.wait_recv()
                else:
                    copy.wait_send()

    def cot_row(ds):
        r0, _ = source_span(ds, 2)
        lr, _ = landing_span(ds, 2)
        k = 0 if ds == -1 else 1
        return remote(
            cot.at[:, pl.ds(r0, 1)], cs.at[1, pl.ds(1, 4), pl.ds(lr, 1)], hs.at[k], hr.at[k], t, s + ds
        )

    for ds in (-1, 1):
        @pl.when(valid(t, s, 0, ds))
        def _(ds=ds):
            cot_row(ds).start()

    keep_tile.wait()
    tmp[...] = jnp.zeros_like(tmp)
    for f in range(4):
        for r in range(2):
            x = cs[1, 1 + f, 1 + r].astype(F32)
            k = f * 2 + r
            tmp[0, pl.ds(k, 1), :] = x[0:1, :]
            tmp[1, pl.ds(k, 1), :] = x[15:16, :]
    col[...] = tmp[...].astype(BF16)

    def cot_col(dt, ds):
        side = 0 if dt == 1 else 1
        k = 2 + side * 3 + ds + 1
        return remote(
            col.at[1 if dt == 1 else 0], colh.at[side, 1 - ds], hs.at[k], hr.at[k], t + dt, s + ds
        )

    for dt in (-1, 1):
        for ds in (-1, 0, 1):
            @pl.when(valid(t, s, dt, ds))
            def _(dt=dt, ds=ds):
                cot_col(dt, ds).start()

    for d in range(4):
        @pl.when(valid(t, s, *SIDES[d]))
        def _(d=d):
            halo_copy(feat, xs.at[1], 0, d, fs, fr).start()

    def gather_cot(j, tt, zd):
        return remote(
            cot.at[:, :, :, pl.ds(pl.multiple_of(zd * 128, 128), 128)],
            cw.at[z, :, :, pl.ds(pl.multiple_of(t * 16, 16), 16), :],
            ws.at[0 if j == 4 else 1], wr.at[0 if j == 4 else 1], tt, group + zd,
        )

    for j in range(1, 8):
        gather_cot(j, core + 2 * lax.rem(pair + j // 4, 2), lax.rem(z + j % 4, ZG)).start()
    keep_cot = pltpu.make_async_copy(
        cot.at[:, :, :, pl.ds(pl.multiple_of(z * 128, 128), 128)],
        cw.at[z, :, :, pl.ds(pl.multiple_of(t * 16, 16), 16), :],
        wsem.at[2],
    )
    keep_cot.start()

    fill_edges(xs, t, s)
    fill_edges(gs, t, s)
    @pl.when(t == 0)
    def _():
        colh[0] = jnp.zeros(colh.shape[1:], BF16)

    @pl.when(t == TM - 1)
    def _():
        colh[1] = jnp.zeros(colh.shape[1:], BF16)

    @pl.when(s == 0)
    def _():
        for side in range(2):
            colh[side, 0] = jnp.zeros(colh.shape[2:], BF16)
        for f in range(4):
            cs[1, 1 + f, 0] = jnp.zeros(cs.shape[3:], BF16)

    @pl.when(s == SPACE - 1)
    def _():
        for side in range(2):
            colh[side, 2] = jnp.zeros(colh.shape[2:], BF16)
        for f in range(4):
            cs[1, 1 + f, 3] = jnp.zeros(cs.shape[3:], BF16)

    @pl.when(group == SPACE - ZG)
    def _():
        edges[1] = jnp.zeros(edges.shape[1:], BF16)

    @pl.when(group == 0)
    def _():
        edges[0] = jnp.zeros(edges.shape[1:], BF16)

    t1[...] = jnp.zeros_like(t1)
    for k in range(27, 32):
        outb[pl.ds(k * 64, 64), :] = jnp.zeros((64, 128), F32)
    for k in range(4):
        zz[k, 0] = jnp.zeros(zz.shape[2:], BF16)
        zz[k, 5] = jnp.zeros(zz.shape[2:], BF16)

    load_wa.wait()
    for n in range(27):
        wt[pl.ds(n * 256, 256), :] = wa[pl.ds(n * 128, 128), :].astype(F32).T.astype(BF16)
    keep_feat.wait()
    fill_shifts(xs, True)
    for ds in (-1, 1):
        @pl.when(valid(t, s, 0, -ds))
        def _(ds=ds):
            cot_row(ds).wait_recv()
    for dt in (-1, 1):
        for ds in (-1, 0, 1):
            @pl.when(valid(t, s, -dt, -ds))
            def _(dt=dt, ds=ds):
                cot_col(dt, ds).wait_recv()
    halo_wait(feat, xs.at[1], 0, (2, 3), fs, fr)
    corners(xs.at[1], fs, fr, "start")
    colf[...] = colh[...].astype(F32)
    index = lax.broadcasted_iota(jnp.int32, (16, 512), 0)
    for f in range(4):
        for r in range(4):
            j = (0, 1, 1, 2)[r]
            k = f * 2 + (1, 0, 1, 0)[r]
            x = cs[1, 1 + f, r].astype(F32)
            left = colf[0, j, pl.ds(k, 1), :]
            right = colf[1, j, pl.ds(k, 1), :]
            cs[0, 1 + f, r] = jnp.where(index == 0, left, pltpu.roll(x, 1, 0)).astype(BF16)
            cs[2, 1 + f, r] = jnp.where(index == 15, right, pltpu.roll(x, 15, 0)).astype(BF16)
    load_wb.wait()
    for b in range(3):
        for c in range(3):
            tile = cs[2 - c, pl.ds(1, 4), pl.ds(2 - b, 2)].reshape(128, 512)
            ct[pl.ds((b * 3 + c) * 512, 512), :] = tile.astype(F32).T.astype(BF16)
    for a in range(3):
        ya[a] = dot(jnp.concatenate([wb[a * 9 + n] for n in range(9)], axis=1), ct[...])
    cell = lax.broadcasted_iota(jnp.int32, (256, 128), 1)
    later = jnp.where(cell < 96, pltpu.roll(ya[0], 96, 1), 0.0)
    earlier = jnp.where(cell >= 32, pltpu.roll(ya[2], 32, 1), 0.0)
    gps[...] = (ya[1] + later + earlier).T.reshape(4, 2, 16, 256).astype(BF16)

    partner = t + 1 - 2 * core

    def forward_cot(y):
        part = cw.at[:, :, :, pl.ds(pl.multiple_of((core + 2 * y) * 16, 16), 16), :]
        return remote(part, part, ws.at[2 + y], wr.at[2 + y], partner, s)

    def give_tile(k):
        tt = lax.rem(t + k, TM)
        return remote(
            gps.at[tt], gpl.at[:, pl.ds(pl.multiple_of(t * 16, 16), 16), :], qs.at[k - 1], qr.at[k - 1], tt, s
        )

    for k in range(1, TM):
        give_tile(k).start()
    gpl[:, pl.ds(pl.multiple_of(t * 16, 16), 16), :] = gps[t]
    wait_bytes(cw.at[0, :, :, pl.ds(0, 16), :], wr.at[0])
    wait_bytes(cw.at[pl.ds(0, 3), :, :, pl.ds(0, 32), :], wr.at[1])
    keep_cot.wait()
    for y in range(2):
        forward_cot(y).start()

    halo_wait(feat, xs.at[1], 0, (0, 1), fs, fr)
    corners(xs.at[1], fs, fr, "recv")
    fill_shifts(xs, False)
    for f in range(2):
        parts = [xs[c, f + a, pl.ds(b, 4)].reshape(512, 128) for a, b, c in TAPS]
        pre[pl.ds(f * 512, 512), :] = dot(jnp.concatenate(parts, axis=1), wa[...])
    for q in range(2):
        summed = jnp.zeros((128, 256), F32)
        for f in range(2):
            for r in range(2):
                rows = pl.ds((f * 4 + q * 2 + r) * 128, 128)
                p = pre[rows, :]
                sig = jax.nn.sigmoid(p)
                summed = summed + p * sig
                pre[rows, :] = sig * (1.0 + p * (1.0 - sig))
        for lane in range(2):
            pool[lane] = summed[:, lane * 128 : lane * 128 + 128]
        for lane in range(2):
            even = pool[lane, pl.ds(0, 64, stride=2), :]
            odd = pool[lane, pl.ds(1, 64, stride=2), :]
            pld[lane, pl.ds(q * 64, 64), :] = (even + odd) * 0.125
    for lane in range(2):
        turned = pld[lane].astype(BF16).astype(F32).T
        for half in range(2):
            block = turned[half * 64 : half * 64 + 64]
            pt[2 * lane + half] = block.astype(BF16)
            top, bottom = (block[0:32], block[32:64])
            edge[0, 2 * lane + half] = jnp.where(low[0:32], top, pltpu.roll(bottom, 64, 1)).astype(BF16)
            edge[1, 2 * lane + half] = jnp.where(low[0:32], pltpu.roll(top, 64, 1), bottom).astype(BF16)

    def give_pooled(tt, ss):
        return remote(pt.at[tt], pz.at[(z + 1) * 4 + t], ps.at[0], pr.at[0], tt, ss)

    def give_edge(tt, ss, k):
        return remote(edge.at[k, tt], edges.at[1 - k, t], ps.at[1 + k], pr.at[2 - k], tt, ss)

    for j in range(1, 16):
        give_pooled(lax.rem(t + j // 4, TM), group + lax.rem(z + j % 4, ZG)).start()
    pz[(z + 1) * 4 + t] = pt[t]

    for k, inside, ss in ((0, jnp.logical_and(z == 0, s > 0), s - 1), (1, jnp.logical_and(z == ZG - 1, s < SPACE - 1), s + 1)):
        @pl.when(inside)
        def _(k=k, ss=ss):
            for j in range(1, TM):
                give_edge(lax.rem(t + j, TM), ss, k).start()
            give_edge(t, ss, k).start()

    for k in range(1, TM):
        give_tile(k).wait_recv()
    for q in range(2):
        u = gpl[q].astype(F32) * 0.125
        for lane in range(2):
            half = u[:, lane * 128 : lane * 128 + 128]
            pool[lane, pl.ds(0, 64, stride=2), :] = half
            pool[lane, pl.ds(1, 64, stride=2), :] = half
        for f in range(2):
            for r in range(2):
                k = f * 4 + q * 2 + r
                for lane in range(2):
                    g = pool[lane] * pre[pl.ds(k * 128, 128), pl.ds(lane * 128, 128)]
                    gs[1, 1 + f, 1 + q * 2 + r, :, pl.ds(lane * 128, 128)] = g.astype(BF16)
                    gt[pl.ds(lane * 128, 128), pl.ds(k * 128, 128)] = g.T.astype(BF16)
    for d in range(4):
        @pl.when(valid(t, s, *SIDES[d]))
        def _(d=d):
            halo_copy(gs.at[1], gs.at[1], 1, d, gsend, grecv).start()

    def pass_edge(k, zd):
        return remote(edges.at[k], edges.at[k], ps.at[3 + k], pr.at[1 + k], t, group + zd)

    def give_pair(m):
        taps = pl.ds(m * 9, 9)
        return remote(pxs.at[taps], pxr.at[taps], xsend.at[m], xrecv.at[m], partner, s)

    for m in range(3):
        rhs = [xs[c, pl.ds(m, 2), pl.ds(b, 4)].reshape(1024, 128) for b in range(3) for c in range(3)]
        res = dot(gt[...], jnp.concatenate(rhs, axis=1))
        for k in range(9):
            outa[pl.ds((m * 9 + k) * 256, 256), :] = res[:, k * 128 : k * 128 + 128]

        def cut_a(k, carry, m=m):
            n = m * 9 + k
            for y in range(2):
                other = pl.multiple_of(n * 256 + (1 - core + 2 * y) * 64, 64)
                pxs[n, y] = outa[pl.ds(other, 64), :].astype(BF16)
            return carry

        lax.fori_loop(0, 9, cut_a, 0)
        give_pair(m).start()
        if m == 1:
            for k, passes in ((0, jnp.logical_and(z == 0, s > 0)), (1, jnp.logical_and(z == ZG - 1, s < SPACE - 1))):
                @pl.when(passes)
                def _(k=k):
                    wait_bytes(edges.at[k], pr.at[1 + k])
                    for j in range(1, ZG):
                        pass_edge(k, lax.rem(z + j, ZG)).start()

    halo_wait(gs.at[1], gs.at[1], 1, (2, 3), gsend, grecv)
    corners(gs.at[1], gsend, grecv, "start")
    fill_shifts(gs, True)

    sx, sy, sz = (s // 8, 2 * lax.rem(s // 4, 2) + pair, z)

    def place(x, y, zed):
        return (core + 2 * lax.rem(y, 2), x * 8 + (y // 2) * 4 + zed)

    coord = (sx, sy, sz)
    for m in range(3):
        give_pair(m).wait_recv()

        def add_pair(i, carry, m=m):
            n = m * 9 + i
            for y in range(2):
                own = pl.multiple_of(n * 256 + (core + 2 * y) * 64, 64)
                su[y] = outa[pl.ds(own, 64), :] + pxr[n, y].astype(F32)
            for v in range(4):
                if m == 0:
                    rows = [su[y, pl.ds(v * 16, 16), :] for y in range(2)]
                elif m == 1:
                    rows = [su[v % 2, pl.ds(x * 16 + (v // 2) * 8, 8), :] for x in range(4)]
                else:
                    rows = [su[y, pl.ds(v * 2 + e, 8, stride=8), :] for y in range(2) for e in range(2)]
                at = pl.ds(pl.multiple_of(i * 32, 32), 32)
                a1[m, v, at, :] = jnp.concatenate(rows, axis=0).astype(BF16)
            return carry

        lax.fori_loop(0, 9, add_pair, 0)
        for k in range(1, 4):
            v = lax.rem(coord[m] + k, 4)
            to = [sx, sy, sz]
            to[m] = v
            remote(a1.at[m, v], r1.at[m, coord[m]], asend.at[m], arecv.at[m], *place(*to)).start()
        r1[m, coord[m]] = a1[m, coord[m]]

    w2 = (pair * 8 + lax.rem(s, 8), sx * 4 + sz, pair * 8 + s // 4)

    def second(m):
        wait_bytes(r1.at[m, pl.ds(0, 3)], arecv.at[m])
        total = r1[m, 0].astype(F32)
        for k in range(1, 4):
            total = total + r1[m, k].astype(F32)
        t1[pl.ds(0, 288), :] = total

        def share_a(j, carry):
            d = lax.rem(w2[m] + j, 16)
            if m == 0:
                q, step, tt, ss = (d * 2, 1, core + 2 * (d // 8), sx * 8 + lax.rem(d, 8))
            elif m == 1:
                q, step, tt, ss = (d * 2, 1, t, (d // 4) * 8 + (sy // 2) * 4 + lax.rem(d, 4))
            else:
                q, step, tt, ss = ((d // 8) * 16 + lax.rem(d, 8), 8, core + 2 * (d // 8), lax.rem(d, 8) * 4 + sz)
            rows = [t1[pl.ds(q + e * step, 16, stride=32), :] for e in range(2)]
            a2[m, d] = jnp.concatenate(rows, axis=0).astype(BF16)

            @pl.when(j > 0)
            def _():
                remote(a2.at[m, d], r2.at[m, w2[m]], asend.at[3 + m], arecv.at[3 + m], tt, ss).start()

            return carry

        lax.fori_loop(0, 16, share_a, 0)
        r2[m, w2[m]] = a2[m, w2[m]]

    for y in range(2):
        forward_cot(y).wait_recv()
    wait_bytes(pz.at[pl.ds(0, 15)], pr.at[0])

    @pl.when(jnp.logical_and(group > 0, z > 0))
    def _():
        wait_bytes(edges.at[0], pr.at[1])

    @pl.when(jnp.logical_and(group < SPACE - ZG, z < ZG - 1))
    def _():
        wait_bytes(edges.at[1], pr.at[2])

    for f in range(4):
        x = edges[0, f].astype(F32)
        pz[f] = jnp.concatenate([pltpu.roll(x, 64, 1), x], axis=0).astype(BF16)
        x = edges[1, f].astype(F32)
        pz[20 + f] = jnp.concatenate([x, pltpu.roll(x, 64, 1)], axis=0).astype(BF16)

    def spread(k, carry):
        block, f = (k // 4, lax.rem(k, 4))
        own = pz[(block + 1) * 4 + f].astype(F32)
        before = pltpu.roll(pz[block * 4 + f].astype(F32), 64, 1)
        after = pltpu.roll(pz[(block + 2) * 4 + f].astype(F32), 64, 1)
        turned = pltpu.roll(own, 64, 1)
        rows = [jnp.where(low, before, turned), own, jnp.where(low, turned, after)]
        for b in range(3):
            x = rows[b]
            cols = [jnp.where(first, 0.0, pltpu.roll(x, 1, 1)), x, jnp.where(last, 0.0, pltpu.roll(x, 127, 1))]
            for c in range(3):
                zz[block, 1 + f, pl.ds((b * 3 + c) * 64, 64), :] = cols[c].astype(BF16)
        return carry

    lax.fori_loop(0, 16, spread, 0)
    for a in range(3):
        lhs = jnp.concatenate([zz[block, f + a] for block in range(4) for f in range(4)], axis=1)
        outb[pl.ds(a * 576, 576), :] = dot(lhs, cw[...].reshape(2048, 128))

    def share_b(j, carry):
        ss = lax.rem(s + j, SPACE)
        o = 2 * ss
        piece = jnp.concatenate([outb[pl.ds(o, 32, stride=64), :], outb[pl.ds(o + 1, 32, stride=64), :]], axis=0)
        sb[ss] = piece.astype(BF16)

        @pl.when(j > 0)
        def _():
            remote(sb.at[ss], rb.at[s], bs, br, t, ss).start()

        return carry

    lax.fori_loop(0, SPACE, share_b, 0)
    rb[s] = sb[s]

    for m in range(3):
        second(m)

    halo_wait(gs.at[1], gs.at[1], 1, (0, 1), gsend, grecv)
    corners(gs.at[1], gsend, grecv, "recv")
    fill_shifts(gs, False)
    for f in range(2):
        parts = [gs[2 - c, f + 2 - a, pl.ds(2 - b, 4)].reshape(512, 256) for a, b, c in TAPS]
        total = dot(jnp.concatenate(parts, axis=1), wt[...])
        gf_out[f] = total.reshape(4, 128, 128).astype(BF16)

    wait_bytes(rb.at[pl.ds(0, 31)], br)
    for k in range(4):
        def add_b(g, total, k=k):
            return total + rb[g * 4 + k].astype(F32)

        fin[...] = lax.fori_loop(0, 8, add_b, jnp.zeros((64, 128), F32))
        for n, (a, b, c) in enumerate(TAPS):
            gb_out[a, b, c, :, pl.ds(k * 128, 128)] = fin[pl.ds(n, 2, stride=32), :]
    for m in range(3):
        wait_bytes(r2.at[m, pl.ds(0, 15)], arecv.at[3 + m])

        def add_a(k, total, m=m):
            return total + r2[m, k].astype(F32)

        fin[pl.ds(0, 32), :] = lax.fori_loop(0, 16, add_a, jnp.zeros((32, 128), F32))
        for b in range(3):
            for c in range(3):
                ga_out[m, b, c] = fin[pl.ds(b * 3 + c, 2, stride=16), :]

    for d in range(4):
        @pl.when(valid(t, s, *SIDES[d]))
        def _(d=d):
            halo_copy(feat, xs.at[1], 0, d, fs, fr).wait_send()
            halo_copy(gs.at[1], gs.at[1], 1, d, gsend, grecv).wait_send()
    corners(xs.at[1], fs, fr, "send")
    corners(gs.at[1], gsend, grecv, "send")
    for ds in (-1, 1):
        @pl.when(valid(t, s, 0, ds))
        def _(ds=ds):
            cot_row(ds).wait_send()
    for dt in (-1, 1):
        for ds in (-1, 0, 1):
            @pl.when(valid(t, s, dt, ds))
            def _(dt=dt, ds=ds):
                cot_col(dt, ds).wait_send()
    wait_bytes(cw.at[0, :, :, pl.ds(0, 16), :], ws.at[0])
    wait_bytes(cw.at[pl.ds(0, 3), :, :, pl.ds(0, 32), :], ws.at[1])
    for y in range(2):
        forward_cot(y).wait_send()
    for k in range(1, TM):
        give_tile(k).wait_send()
    wait_bytes(pz.at[pl.ds(0, 15)], ps.at[0])

    @pl.when(jnp.logical_and(z == 0, s > 0))
    def _():
        wait_bytes(edges.at[0], ps.at[1])
        wait_bytes(pz.at[pl.ds(0, 6)], ps.at[3])

    @pl.when(jnp.logical_and(z == ZG - 1, s < SPACE - 1))
    def _():
        wait_bytes(edges.at[0], ps.at[2])
        wait_bytes(pz.at[pl.ds(0, 6)], ps.at[4])

    for m in range(3):
        give_pair(m).wait_send()
        wait_bytes(r1.at[m, pl.ds(0, 3)], asend.at[m])
        wait_bytes(r2.at[m, pl.ds(0, 15)], asend.at[3 + m])
    wait_bytes(rb.at[pl.ds(0, 31)], bs)


def shards(features, weight_a, weight_b, cotangent):
    vmem = pl.BlockSpec(memory_space=pltpu.VMEM)
    far = pl.BlockSpec(memory_space=pl.ANY)
    dma = pltpu.SemaphoreType.DMA
    gf, ga, gb = pl.pallas_call(
        body,
        out_shape=(
            jax.ShapeDtypeStruct((2, 4, 128, 128), BF16),
            jax.ShapeDtypeStruct((3, 3, 3, 2, 128), F32),
            jax.ShapeDtypeStruct((3, 3, 3, 2, 512), F32),
        ),
        in_specs=[far, far, far, far],
        out_specs=(vmem, vmem, vmem),
        scratch_shapes=[
            pltpu.VMEM((3456, 256), BF16),
            pltpu.VMEM((27, 256, 512), BF16),
            pltpu.VMEM((3, 4, 6, 128, 128), BF16),
            pltpu.VMEM((3, 6, 4, 16, 512), BF16),
            pltpu.VMEM((4, 4, 2, 64, 128), BF16),
            pltpu.VMEM((2, 16, 512), BF16),
            pltpu.VMEM((2, 3, 16, 512), BF16),
            pltpu.VMEM((2, 3, 16, 512), F32),
            pltpu.VMEM((4, 2, 16, 256), BF16),
            pltpu.VMEM((2, 64, 256), BF16),
            pltpu.VMEM((1024, 256), F32),
            pltpu.VMEM((2, 128, 128), F32),
            pltpu.VMEM((4, 64, 128), BF16),
            pltpu.VMEM((24, 64, 128), BF16),
            pltpu.VMEM((3, 4, 6, 128, 256), BF16),
            pltpu.VMEM((256, 1024), BF16),
            pltpu.VMEM((4, 6, 576, 128), BF16),
            pltpu.VMEM((6912, 128), F32),
            pltpu.VMEM((2048, 128), F32),
            pltpu.VMEM((32, 64, 128), BF16),
            pltpu.VMEM((32, 64, 128), BF16),
            pltpu.VMEM((27, 2, 64, 128), BF16),
            pltpu.VMEM((27, 2, 64, 128), BF16),
            pltpu.VMEM((2, 64, 128), F32),
            pltpu.VMEM((3, 4, 288, 128), BF16),
            pltpu.VMEM((3, 4, 288, 128), BF16),
            pltpu.VMEM((512, 128), F32),
            pltpu.VMEM((3, 16, 32, 128), BF16),
            pltpu.VMEM((3, 16, 32, 128), BF16),
            pltpu.VMEM((2, 16, 512), F32),
            pltpu.VMEM((2, 128, 128), F32),
            pltpu.VMEM((2, 4, 32, 128), BF16),
            pltpu.VMEM((2, 4, 32, 128), BF16),
            pltpu.VMEM((64, 128), F32),
            pltpu.VMEM((4608, 128), BF16),
            pltpu.VMEM((3, 256, 128), F32),
            pltpu.VMEM((6912, 128), BF16),
            dma((5,)), dma((8,)), dma((8,)), dma((8,)), dma((8,)), dma((4,)), dma((4,)),
            dma((3,)), dma((3,)), dma((5,)), dma((3,)), dma((8,)), dma((8,)),
            dma, dma, dma((3,)), dma((3,)), dma((6,)), dma((6,)),
        ],
        compiler_params=pltpu.CompilerParams(collective_id=0, has_side_effects=True, vmem_limit_bytes=56 * 2**20),
    )(features, weight_a.reshape(3456, 256), weight_b.reshape(27, 256, 512), cotangent)
    return (gf, ga.transpose(0, 1, 2, 4, 3), gb)


def solution(mesh):
    placed = (P("tm", "space", None, None), P(), P(), P(None, "space", "tm", None))
    return jax.shard_map(
        shards,
        mesh=mesh,
        in_specs=placed,
        out_specs=(
            P("tm", "space", None, None),
            P(None, None, None, None, ("tm", "space")),
            P(None, None, None, ("tm", "space"), None),
        ),
        check_vma=False,
    )
```

```python
import jax
import jax.numpy as jnp
from jax import lax
from jax.experimental import pallas as pl
from jax.experimental.pallas import tpu as pltpu
from jax.sharding import PartitionSpec as P

F32 = jnp.float32
BF16 = jnp.bfloat16
MESH = pl.DeviceIdType.MESH
TM = 4
SPACE = 32
ZG = 4
SIDES = [(-1, 0), (1, 0), (0, -1), (0, 1)]
CORNERS = [(dt, ds) for dt in (-1, 1) for ds in (-1, 1)]
TAPS = [(a, b, c) for a in range(3) for b in range(3) for c in range(3)]
NT = (((1,), (1,)), ((), ()))


def dot(a, b):
    return lax.dot_general(a, b, (((1,), (0,)), ((), ())), preferred_element_type=F32)


def dot_nt(a, b):
    return lax.dot_general(a, b, NT, preferred_element_type=F32)


def valid(t, s, dt, ds):
    ok = jnp.bool_(True)
    if dt == 1:
        ok = t < TM - 1
    if dt == -1:
        ok = t > 0
    if ds == 1:
        ok = jnp.logical_and(ok, s < SPACE - 1)
    if ds == -1:
        ok = jnp.logical_and(ok, s > 0)
    return ok


def source_span(d, size):
    return (0, size) if d == 0 else ((size - 1, 1) if d == 1 else (0, 1))


def landing_span(d, size):
    return (1, size) if d == 0 else ((0, 1) if d == 1 else (size + 1, 1))


def shift_rows(x, step):
    rows = x.shape[0]
    index = lax.broadcasted_iota(jnp.int32, x.shape, 0)
    if step == 1:
        return jnp.where(index == 0, 0.0, pltpu.roll(x, 1, 0))
    return jnp.where(index == rows - 1, 0.0, pltpu.roll(x, rows - 1, 0))


def fill_edges(buf, t, s):
    @pl.when(t == 0)
    def _():
        buf[1, 0] = jnp.zeros(buf.shape[2:], BF16)

    @pl.when(t == TM - 1)
    def _():
        buf[1, 3] = jnp.zeros(buf.shape[2:], BF16)

    @pl.when(s == 0)
    def _():
        for f in range(4):
            buf[1, f, 0] = jnp.zeros(buf.shape[3:], BF16)

    @pl.when(s == SPACE - 1)
    def _():
        for f in range(4):
            buf[1, f, 5] = jnp.zeros(buf.shape[3:], BF16)


def fill_shifts(buf, own):
    def shift(f, r):
        x = buf[1, f, r].astype(F32)
        buf[0, f, r] = shift_rows(x, 1).astype(BF16)
        buf[2, f, r] = shift_rows(x, -1).astype(BF16)

    def inner(k, carry):
        shift(1 + k // 4, 1 + lax.rem(k, 4))
        return carry

    def frames(k, carry):
        shift(3 * (k // 6), lax.rem(k, 6))
        return carry

    def rows(k, carry):
        shift(1 + k // 2, 5 * lax.rem(k, 2))
        return carry

    if own:
        lax.fori_loop(0, 8, inner, 0)
    else:
        lax.fori_loop(0, 12, frames, 0)
        lax.fori_loop(0, 4, rows, 0)


def body(
    feat, wa_hbm, wb_hbm, cot,
    gf_out, ga_out, gb_out,
    wa, wb, xs, cs, cw, col, colh, colf, gps, gpl, pre, pool, pt, pz, gs, gt, zz, outa, outb,
    sb, rb, pxs, pxr, su, a1, r1, t1, a2, r2, tmp, pld, edge, edges, fin, ct, ya, wt,
    wsem, fs, fr, hs, hr, ws, wr, qs, qr, ps, pr, gsend, grecv, bs, br, xsend, xrecv, asend, arecv,
):
    t = lax.axis_index("tm")
    s = lax.axis_index("space")
    z = lax.rem(s, ZG)
    group = s - z
    core = lax.rem(t, 2)
    pair = t // 2

    def remote(src, dst, send, recv, tt, ss):
        return pltpu.make_async_remote_copy(
            src_ref=src, dst_ref=dst, send_sem=send, recv_sem=recv, device_id=(tt, ss), device_id_type=MESH
        )

    def wait_bytes(ref, sem):
        pltpu.make_async_copy(ref, ref, sem).wait()

    load_wa = pltpu.make_async_copy(wa_hbm, wa, wsem.at[0])
    load_wb = pltpu.make_async_copy(wb_hbm, wb, wsem.at[1])
    keep_tile = pltpu.make_async_copy(cot, cs.at[1, pl.ds(1, 4), pl.ds(1, 2)], wsem.at[3])
    keep_feat = pltpu.make_async_copy(feat, xs.at[1, pl.ds(1, 2), pl.ds(1, 4)], wsem.at[4])
    keep_tile.start()
    keep_feat.start()
    load_wa.start()
    load_wb.start()

    barrier = pltpu.get_barrier_semaphore()

    def greet(tt, ss):
        pl.semaphore_signal(barrier, inc=1, device_id=(tt, ss), device_id_type=MESH)

    def greet_near(j, carry):
        ss = group - ZG + lax.rem(j, 12)

        @pl.when(jnp.logical_and(ss >= 0, ss < SPACE))
        def _():
            greet(1 - core + 2 * (j // 12), ss)

        return carry

    def greet_far(j, carry):
        @pl.when(j > 0)
        def _():
            greet(core + 2 * lax.rem(pair + j // 32, 2), lax.rem(s + j, SPACE))

        return carry

    lax.fori_loop(0, 24, greet_near, 0)
    lax.fori_loop(0, 64, greet_far, 0)
    greeted = 63 + 24 - jnp.where(group == 0, 8, 0) - jnp.where(group == SPACE - ZG, 8, 0)

    pl.semaphore_wait(barrier, greeted)

    lane_id = lax.broadcasted_iota(jnp.int32, (64, 128), 1)
    low = lane_id < 64
    first = lax.rem(lane_id, 64) == 0
    last = lax.rem(lane_id, 64) == 63

    def halo_copy(source, target, base, d, send, recv):
        dt, ds = SIDES[d]
        f0, fn = source_span(dt, 2)
        r0, rn = source_span(ds, 4)
        lf, _ = landing_span(dt, 2)
        lr, _ = landing_span(ds, 4)
        return remote(
            source.at[pl.ds(base + f0, fn), pl.ds(base + r0, rn)],
            target.at[pl.ds(lf, fn), pl.ds(lr, rn)],
            send.at[d], recv.at[d], t + dt, s + ds,
        )

    def halo_wait(source, target, base, ways, send, recv):
        for d in ways:
            dt, ds = SIDES[d]

            @pl.when(valid(t, s, -dt, -ds))
            def _(d=d):
                halo_copy(source, target, base, d, send, recv).wait_recv()

    def corner_copy(target, d, send, recv):
        dt, ds = CORNERS[d]
        row = pl.ds(0 if ds == 1 else 5, 1)
        return remote(
            target.at[pl.ds(2 if dt == 1 else 1, 1), row],
            target.at[pl.ds(0 if dt == 1 else 3, 1), row],
            send.at[4 + d], recv.at[4 + d], t + dt, s,
        )

    def corner_valid(d, arriving):
        dt, ds = CORNERS[d]
        return jnp.logical_and(valid(t, s, -dt if arriving else dt, 0), valid(t, s, 0, -ds))

    def corners(target, send, recv, what):
        for d in range(4):
            @pl.when(corner_valid(d, what == "recv"))
            def _(d=d):
                copy = corner_copy(target, d, send, recv)
                if what == "start":
                    copy.start()
                elif what == "recv":
                    copy.wait_recv()
                else:
                    copy.wait_send()

    def cot_row(ds):
        r0, _ = source_span(ds, 2)
        lr, _ = landing_span(ds, 2)
        k = 0 if ds == -1 else 1
        return remote(
            cot.at[:, pl.ds(r0, 1)], cs.at[1, pl.ds(1, 4), pl.ds(lr, 1)], hs.at[k], hr.at[k], t, s + ds
        )

    for ds in (-1, 1):
        @pl.when(valid(t, s, 0, ds))
        def _(ds=ds):
            cot_row(ds).start()

    keep_tile.wait()
    tmp[...] = jnp.zeros_like(tmp)
    for f in range(4):
        for r in range(2):
            x = cs[1, 1 + f, 1 + r].astype(F32)
            k = f * 2 + r
            tmp[0, pl.ds(k, 1), :] = x[0:1, :]
            tmp[1, pl.ds(k, 1), :] = x[15:16, :]
    col[...] = tmp[...].astype(BF16)

    def cot_col(dt, ds):
        side = 0 if dt == 1 else 1
        k = 2 + side * 3 + ds + 1
        return remote(
            col.at[1 if dt == 1 else 0], colh.at[side, 1 - ds], hs.at[k], hr.at[k], t + dt, s + ds
        )

    for dt in (-1, 1):
        for ds in (-1, 0, 1):
            @pl.when(valid(t, s, dt, ds))
            def _(dt=dt, ds=ds):
                cot_col(dt, ds).start()

    for d in range(4):
        @pl.when(valid(t, s, *SIDES[d]))
        def _(d=d):
            halo_copy(feat, xs.at[1], 0, d, fs, fr).start()

    def gather_cot(j, tt, zd):
        return remote(
            cot.at[:, :, :, pl.ds(pl.multiple_of(zd * 128, 128), 128)],
            cw.at[z, :, :, pl.ds(pl.multiple_of(t * 16, 16), 16), :],
            ws.at[0 if j == 4 else 1], wr.at[0 if j == 4 else 1], tt, group + zd,
        )

    for j in range(1, 8):
        gather_cot(j, core + 2 * lax.rem(pair + j // 4, 2), lax.rem(z + j % 4, ZG)).start()
    keep_cot = pltpu.make_async_copy(
        cot.at[:, :, :, pl.ds(pl.multiple_of(z * 128, 128), 128)],
        cw.at[z, :, :, pl.ds(pl.multiple_of(t * 16, 16), 16), :],
        wsem.at[2],
    )
    keep_cot.start()

    fill_edges(xs, t, s)
    fill_edges(gs, t, s)
    @pl.when(t == 0)
    def _():
        colh[0] = jnp.zeros(colh.shape[1:], BF16)

    @pl.when(t == TM - 1)
    def _():
        colh[1] = jnp.zeros(colh.shape[1:], BF16)

    @pl.when(s == 0)
    def _():
        for side in range(2):
            colh[side, 0] = jnp.zeros(colh.shape[2:], BF16)
        for f in range(4):
            cs[1, 1 + f, 0] = jnp.zeros(cs.shape[3:], BF16)

    @pl.when(s == SPACE - 1)
    def _():
        for side in range(2):
            colh[side, 2] = jnp.zeros(colh.shape[2:], BF16)
        for f in range(4):
            cs[1, 1 + f, 3] = jnp.zeros(cs.shape[3:], BF16)

    @pl.when(group == SPACE - ZG)
    def _():
        edges[1] = jnp.zeros(edges.shape[1:], BF16)

    @pl.when(group == 0)
    def _():
        edges[0] = jnp.zeros(edges.shape[1:], BF16)

    t1[...] = jnp.zeros_like(t1)
    for k in range(27, 32):
        outb[pl.ds(k * 64, 64), :] = jnp.zeros((64, 128), F32)
    for k in range(4):
        zz[k, 0] = jnp.zeros(zz.shape[2:], BF16)
        zz[k, 5] = jnp.zeros(zz.shape[2:], BF16)

    load_wa.wait()
    keep_feat.wait()
    fill_shifts(xs, True)
    for ds in (-1, 1):
        @pl.when(valid(t, s, 0, -ds))
        def _(ds=ds):
            cot_row(ds).wait_recv()
    for dt in (-1, 1):
        for ds in (-1, 0, 1):
            @pl.when(valid(t, s, -dt, -ds))
            def _(dt=dt, ds=ds):
                cot_col(dt, ds).wait_recv()
    halo_wait(feat, xs.at[1], 0, (2, 3), fs, fr)
    corners(xs.at[1], fs, fr, "start")
    colf[...] = colh[...].astype(F32)
    index = lax.broadcasted_iota(jnp.int32, (16, 512), 0)
    for f in range(4):
        for r in range(4):
            j = (0, 1, 1, 2)[r]
            k = f * 2 + (1, 0, 1, 0)[r]
            x = cs[1, 1 + f, r].astype(F32)
            left = colf[0, j, pl.ds(k, 1), :]
            right = colf[1, j, pl.ds(k, 1), :]
            cs[0, 1 + f, r] = jnp.where(index == 0, left, pltpu.roll(x, 1, 0)).astype(BF16)
            cs[2, 1 + f, r] = jnp.where(index == 15, right, pltpu.roll(x, 15, 0)).astype(BF16)
    load_wb.wait()
    for b in range(3):
        for c in range(3):
            tile = cs[2 - c, pl.ds(1, 4), pl.ds(2 - b, 2)].reshape(128, 512)
            ct[pl.ds((b * 3 + c) * 512, 512), :] = tile.astype(F32).T.astype(BF16)
    for a in range(3):
        ya[a] = dot(jnp.concatenate([wb[a * 9 + n] for n in range(9)], axis=1), ct[...])
    cell = lax.broadcasted_iota(jnp.int32, (256, 128), 1)
    later = jnp.where(cell < 96, pltpu.roll(ya[0], 96, 1), 0.0)
    earlier = jnp.where(cell >= 32, pltpu.roll(ya[2], 32, 1), 0.0)
    gps[...] = (ya[1] + later + earlier).T.reshape(4, 2, 16, 256).astype(BF16)

    partner = t + 1 - 2 * core

    def forward_cot(y):
        part = cw.at[:, :, :, pl.ds(pl.multiple_of((core + 2 * y) * 16, 16), 16), :]
        return remote(part, part, ws.at[2 + y], wr.at[2 + y], partner, s)

    def give_tile(k):
        tt = lax.rem(t + k, TM)
        return remote(
            gps.at[tt], gpl.at[:, pl.ds(pl.multiple_of(t * 16, 16), 16), :], qs.at[k - 1], qr.at[k - 1], tt, s
        )

    for k in range(1, TM):
        give_tile(k).start()
    gpl[:, pl.ds(pl.multiple_of(t * 16, 16), 16), :] = gps[t]
    wait_bytes(cw.at[0, :, :, pl.ds(0, 16), :], wr.at[0])
    wait_bytes(cw.at[pl.ds(0, 3), :, :, pl.ds(0, 32), :], wr.at[1])
    keep_cot.wait()
    for y in range(2):
        forward_cot(y).start()

    halo_wait(feat, xs.at[1], 0, (0, 1), fs, fr)
    corners(xs.at[1], fs, fr, "recv")
    fill_shifts(xs, False)
    for f in range(2):
        parts = [xs[c, f + a, pl.ds(b, 4)].reshape(512, 128) for a, b, c in TAPS]
        pre[pl.ds(f * 512, 512), :] = dot(jnp.concatenate(parts, axis=1), wa[...])
    for q in range(2):
        summed = jnp.zeros((128, 256), F32)
        for f in range(2):
            for r in range(2):
                rows = pl.ds((f * 4 + q * 2 + r) * 128, 128)
                p = pre[rows, :]
                sig = jax.nn.sigmoid(p)
                summed = summed + p * sig
                pre[rows, :] = sig * (1.0 + p * (1.0 - sig))
        for lane in range(2):
            pool[lane] = summed[:, lane * 128 : lane * 128 + 128]
        for lane in range(2):
            even = pool[lane, pl.ds(0, 64, stride=2), :]
            odd = pool[lane, pl.ds(1, 64, stride=2), :]
            pld[lane, pl.ds(q * 64, 64), :] = (even + odd) * 0.125
    for lane in range(2):
        turned = pld[lane].astype(BF16).astype(F32).T
        for half in range(2):
            block = turned[half * 64 : half * 64 + 64]
            pt[2 * lane + half] = block.astype(BF16)
            top, bottom = (block[0:32], block[32:64])
            edge[0, 2 * lane + half] = jnp.where(low[0:32], top, pltpu.roll(bottom, 64, 1)).astype(BF16)
            edge[1, 2 * lane + half] = jnp.where(low[0:32], pltpu.roll(top, 64, 1), bottom).astype(BF16)

    def give_pooled(tt, ss):
        return remote(pt.at[tt], pz.at[(z + 1) * 4 + t], ps.at[0], pr.at[0], tt, ss)

    def give_edge(tt, ss, k):
        return remote(edge.at[k, tt], edges.at[1 - k, t], ps.at[1 + k], pr.at[2 - k], tt, ss)

    for j in range(1, 16):
        give_pooled(lax.rem(t + j // 4, TM), group + lax.rem(z + j % 4, ZG)).start()
    pz[(z + 1) * 4 + t] = pt[t]

    for k, inside, ss in ((0, jnp.logical_and(z == 0, s > 0), s - 1), (1, jnp.logical_and(z == ZG - 1, s < SPACE - 1), s + 1)):
        @pl.when(inside)
        def _(k=k, ss=ss):
            for j in range(1, TM):
                give_edge(lax.rem(t + j, TM), ss, k).start()
            give_edge(t, ss, k).start()

    for k in range(1, TM):
        give_tile(k).wait_recv()
    for q in range(2):
        u = gpl[q].astype(F32) * 0.125
        for lane in range(2):
            half = u[:, lane * 128 : lane * 128 + 128]
            pool[lane, pl.ds(0, 64, stride=2), :] = half
            pool[lane, pl.ds(1, 64, stride=2), :] = half
        for f in range(2):
            for r in range(2):
                k = f * 4 + q * 2 + r
                for lane in range(2):
                    g = pool[lane] * pre[pl.ds(k * 128, 128), pl.ds(lane * 128, 128)]
                    gs[1, 1 + f, 1 + q * 2 + r, :, pl.ds(lane * 128, 128)] = g.astype(BF16)
                    gt[pl.ds(lane * 128, 128), pl.ds(k * 128, 128)] = g.T.astype(BF16)
    for d in range(4):
        @pl.when(valid(t, s, *SIDES[d]))
        def _(d=d):
            halo_copy(gs.at[1], gs.at[1], 1, d, gsend, grecv).start()

    def pass_edge(k, zd):
        return remote(edges.at[k], edges.at[k], ps.at[3 + k], pr.at[1 + k], t, group + zd)

    def give_pair(m):
        taps = pl.ds(m * 9, 9)
        return remote(pxs.at[taps], pxr.at[taps], xsend.at[m], xrecv.at[m], partner, s)

    for m in range(3):
        rhs = [xs[c, pl.ds(m, 2), pl.ds(b, 4)].reshape(1024, 128) for b in range(3) for c in range(3)]
        res = dot(gt[...], jnp.concatenate(rhs, axis=1))
        for k in range(9):
            outa[pl.ds((m * 9 + k) * 256, 256), :] = res[:, k * 128 : k * 128 + 128]

        def cut_a(k, carry, m=m):
            n = m * 9 + k
            for y in range(2):
                other = pl.multiple_of(n * 256 + (1 - core + 2 * y) * 64, 64)
                pxs[n, y] = outa[pl.ds(other, 64), :].astype(BF16)
            return carry

        lax.fori_loop(0, 9, cut_a, 0)
        give_pair(m).start()
        if m == 1:
            for k, passes in ((0, jnp.logical_and(z == 0, s > 0)), (1, jnp.logical_and(z == ZG - 1, s < SPACE - 1))):
                @pl.when(passes)
                def _(k=k):
                    wait_bytes(edges.at[k], pr.at[1 + k])
                    for j in range(1, ZG):
                        pass_edge(k, lax.rem(z + j, ZG)).start()

    halo_wait(gs.at[1], gs.at[1], 1, (2, 3), gsend, grecv)
    corners(gs.at[1], gsend, grecv, "start")
    fill_shifts(gs, True)

    sx, sy, sz = (s // 8, 2 * lax.rem(s // 4, 2) + pair, z)

    def place(x, y, zed):
        return (core + 2 * lax.rem(y, 2), x * 8 + (y // 2) * 4 + zed)

    coord = (sx, sy, sz)
    for m in range(3):
        give_pair(m).wait_recv()

        def add_pair(i, carry, m=m):
            n = m * 9 + i
            for y in range(2):
                own = pl.multiple_of(n * 256 + (core + 2 * y) * 64, 64)
                su[y] = outa[pl.ds(own, 64), :] + pxr[n, y].astype(F32)
            for v in range(4):
                if m == 0:
                    rows = [su[y, pl.ds(v * 16, 16), :] for y in range(2)]
                elif m == 1:
                    rows = [su[v % 2, pl.ds(x * 16 + (v // 2) * 8, 8), :] for x in range(4)]
                else:
                    rows = [su[y, pl.ds(v * 2 + e, 8, stride=8), :] for y in range(2) for e in range(2)]
                at = pl.ds(pl.multiple_of(i * 32, 32), 32)
                a1[m, v, at, :] = jnp.concatenate(rows, axis=0).astype(BF16)
            return carry

        lax.fori_loop(0, 9, add_pair, 0)
        for k in range(1, 4):
            v = lax.rem(coord[m] + k, 4)
            to = [sx, sy, sz]
            to[m] = v
            remote(a1.at[m, v], r1.at[m, coord[m]], asend.at[m], arecv.at[m], *place(*to)).start()
        r1[m, coord[m]] = a1[m, coord[m]]

    w2 = (pair * 8 + lax.rem(s, 8), sx * 4 + sz, pair * 8 + s // 4)

    def second(m):
        wait_bytes(r1.at[m, pl.ds(0, 3)], arecv.at[m])
        total = r1[m, 0].astype(F32)
        for k in range(1, 4):
            total = total + r1[m, k].astype(F32)
        t1[pl.ds(0, 288), :] = total

        def share_a(j, carry):
            d = lax.rem(w2[m] + j, 16)
            if m == 0:
                q, step, tt, ss = (d * 2, 1, core + 2 * (d // 8), sx * 8 + lax.rem(d, 8))
            elif m == 1:
                q, step, tt, ss = (d * 2, 1, t, (d // 4) * 8 + (sy // 2) * 4 + lax.rem(d, 4))
            else:
                q, step, tt, ss = ((d // 8) * 16 + lax.rem(d, 8), 8, core + 2 * (d // 8), lax.rem(d, 8) * 4 + sz)
            rows = [t1[pl.ds(q + e * step, 16, stride=32), :] for e in range(2)]
            a2[m, d] = jnp.concatenate(rows, axis=0).astype(BF16)

            @pl.when(j > 0)
            def _():
                remote(a2.at[m, d], r2.at[m, w2[m]], asend.at[3 + m], arecv.at[3 + m], tt, ss).start()

            return carry

        lax.fori_loop(0, 16, share_a, 0)
        r2[m, w2[m]] = a2[m, w2[m]]

    for y in range(2):
        forward_cot(y).wait_recv()
    wait_bytes(pz.at[pl.ds(0, 15)], pr.at[0])

    @pl.when(jnp.logical_and(group > 0, z > 0))
    def _():
        wait_bytes(edges.at[0], pr.at[1])

    @pl.when(jnp.logical_and(group < SPACE - ZG, z < ZG - 1))
    def _():
        wait_bytes(edges.at[1], pr.at[2])

    for f in range(4):
        x = edges[0, f].astype(F32)
        pz[f] = jnp.concatenate([pltpu.roll(x, 64, 1), x], axis=0).astype(BF16)
        x = edges[1, f].astype(F32)
        pz[20 + f] = jnp.concatenate([x, pltpu.roll(x, 64, 1)], axis=0).astype(BF16)

    def spread(k, carry):
        block, f = (k // 4, lax.rem(k, 4))
        own = pz[(block + 1) * 4 + f].astype(F32)
        before = pltpu.roll(pz[block * 4 + f].astype(F32), 64, 1)
        after = pltpu.roll(pz[(block + 2) * 4 + f].astype(F32), 64, 1)
        turned = pltpu.roll(own, 64, 1)
        rows = [jnp.where(low, before, turned), own, jnp.where(low, turned, after)]
        for b in range(3):
            x = rows[b]
            cols = [jnp.where(first, 0.0, pltpu.roll(x, 1, 1)), x, jnp.where(last, 0.0, pltpu.roll(x, 127, 1))]
            for c in range(3):
                zz[block, 1 + f, pl.ds((b * 3 + c) * 64, 64), :] = cols[c].astype(BF16)
        return carry

    lax.fori_loop(0, 16, spread, 0)
    for a in range(3):
        lhs = jnp.concatenate([zz[block, f + a] for block in range(4) for f in range(4)], axis=1)
        outb[pl.ds(a * 576, 576), :] = dot(lhs, cw[...].reshape(2048, 128))

    def share_b(j, carry):
        ss = lax.rem(s + j, SPACE)
        o = 2 * ss
        piece = jnp.concatenate([outb[pl.ds(o, 32, stride=64), :], outb[pl.ds(o + 1, 32, stride=64), :]], axis=0)
        sb[ss] = piece.astype(BF16)

        @pl.when(j > 0)
        def _():
            remote(sb.at[ss], rb.at[s], bs, br, t, ss).start()

        return carry

    lax.fori_loop(0, SPACE, share_b, 0)
    rb[s] = sb[s]

    for m in range(3):
        second(m)

    for n in range(27):
        wt[pl.ds(n * 256, 256), :] = wa[pl.ds(n * 128, 128), :].astype(F32).T.astype(BF16)
    halo_wait(gs.at[1], gs.at[1], 1, (0, 1), gsend, grecv)
    corners(gs.at[1], gsend, grecv, "recv")
    fill_shifts(gs, False)
    for f in range(2):
        parts = [gs[2 - c, f + 2 - a, pl.ds(2 - b, 4)].reshape(512, 256) for a, b, c in TAPS]
        total = dot(jnp.concatenate(parts, axis=1), wt[...])
        gf_out[f] = total.reshape(4, 128, 128).astype(BF16)

    wait_bytes(rb.at[pl.ds(0, 31)], br)
    for k in range(4):
        def add_b(g, total, k=k):
            return total + rb[g * 4 + k].astype(F32)

        fin[...] = lax.fori_loop(0, 8, add_b, jnp.zeros((64, 128), F32))
        for n, (a, b, c) in enumerate(TAPS):
            gb_out[a, b, c, :, pl.ds(k * 128, 128)] = fin[pl.ds(n, 2, stride=32), :]
    for m in range(3):
        wait_bytes(r2.at[m, pl.ds(0, 15)], arecv.at[3 + m])

        def add_a(k, total, m=m):
            return total + r2[m, k].astype(F32)

        fin[pl.ds(0, 32), :] = lax.fori_loop(0, 16, add_a, jnp.zeros((32, 128), F32))
        for b in range(3):
            for c in range(3):
                ga_out[m, b, c] = fin[pl.ds(b * 3 + c, 2, stride=16), :]

    for d in range(4):
        @pl.when(valid(t, s, *SIDES[d]))
        def _(d=d):
            halo_copy(feat, xs.at[1], 0, d, fs, fr).wait_send()
            halo_copy(gs.at[1], gs.at[1], 1, d, gsend, grecv).wait_send()
    corners(xs.at[1], fs, fr, "send")
    corners(gs.at[1], gsend, grecv, "send")
    for ds in (-1, 1):
        @pl.when(valid(t, s, 0, ds))
        def _(ds=ds):
            cot_row(ds).wait_send()
    for dt in (-1, 1):
        for ds in (-1, 0, 1):
            @pl.when(valid(t, s, dt, ds))
            def _(dt=dt, ds=ds):
                cot_col(dt, ds).wait_send()
    wait_bytes(cw.at[0, :, :, pl.ds(0, 16), :], ws.at[0])
    wait_bytes(cw.at[pl.ds(0, 3), :, :, pl.ds(0, 32), :], ws.at[1])
    for y in range(2):
        forward_cot(y).wait_send()
    for k in range(1, TM):
        give_tile(k).wait_send()
    wait_bytes(pz.at[pl.ds(0, 15)], ps.at[0])

    @pl.when(jnp.logical_and(z == 0, s > 0))
    def _():
        wait_bytes(edges.at[0], ps.at[1])
        wait_bytes(pz.at[pl.ds(0, 6)], ps.at[3])

    @pl.when(jnp.logical_and(z == ZG - 1, s < SPACE - 1))
    def _():
        wait_bytes(edges.at[0], ps.at[2])
        wait_bytes(pz.at[pl.ds(0, 6)], ps.at[4])

    for m in range(3):
        give_pair(m).wait_send()
        wait_bytes(r1.at[m, pl.ds(0, 3)], asend.at[m])
        wait_bytes(r2.at[m, pl.ds(0, 15)], asend.at[3 + m])
    wait_bytes(rb.at[pl.ds(0, 31)], bs)


def shards(features, weight_a, weight_b, cotangent):
    vmem = pl.BlockSpec(memory_space=pltpu.VMEM)
    far = pl.BlockSpec(memory_space=pl.ANY)
    dma = pltpu.SemaphoreType.DMA
    gf, ga, gb = pl.pallas_call(
        body,
        out_shape=(
            jax.ShapeDtypeStruct((2, 4, 128, 128), BF16),
            jax.ShapeDtypeStruct((3, 3, 3, 2, 128), F32),
            jax.ShapeDtypeStruct((3, 3, 3, 2, 512), F32),
        ),
        in_specs=[far, far, far, far],
        out_specs=(vmem, vmem, vmem),
        scratch_shapes=[
            pltpu.VMEM((3456, 256), BF16),
            pltpu.VMEM((27, 256, 512), BF16),
            pltpu.VMEM((3, 4, 6, 128, 128), BF16),
            pltpu.VMEM((3, 6, 4, 16, 512), BF16),
            pltpu.VMEM((4, 4, 2, 64, 128), BF16),
            pltpu.VMEM((2, 16, 512), BF16),
            pltpu.VMEM((2, 3, 16, 512), BF16),
            pltpu.VMEM((2, 3, 16, 512), F32),
            pltpu.VMEM((4, 2, 16, 256), BF16),
            pltpu.VMEM((2, 64, 256), BF16),
            pltpu.VMEM((1024, 256), F32),
            pltpu.VMEM((2, 128, 128), F32),
            pltpu.VMEM((4, 64, 128), BF16),
            pltpu.VMEM((24, 64, 128), BF16),
            pltpu.VMEM((3, 4, 6, 128, 256), BF16),
            pltpu.VMEM((256, 1024), BF16),
            pltpu.VMEM((4, 6, 576, 128), BF16),
            pltpu.VMEM((6912, 128), F32),
            pltpu.VMEM((2048, 128), F32),
            pltpu.VMEM((32, 64, 128), BF16),
            pltpu.VMEM((32, 64, 128), BF16),
            pltpu.VMEM((27, 2, 64, 128), BF16),
            pltpu.VMEM((27, 2, 64, 128), BF16),
            pltpu.VMEM((2, 64, 128), F32),
            pltpu.VMEM((3, 4, 288, 128), BF16),
            pltpu.VMEM((3, 4, 288, 128), BF16),
            pltpu.VMEM((512, 128), F32),
            pltpu.VMEM((3, 16, 32, 128), BF16),
            pltpu.VMEM((3, 16, 32, 128), BF16),
            pltpu.VMEM((2, 16, 512), F32),
            pltpu.VMEM((2, 128, 128), F32),
            pltpu.VMEM((2, 4, 32, 128), BF16),
            pltpu.VMEM((2, 4, 32, 128), BF16),
            pltpu.VMEM((64, 128), F32),
            pltpu.VMEM((4608, 128), BF16),
            pltpu.VMEM((3, 256, 128), F32),
            pltpu.VMEM((6912, 128), BF16),
            dma((5,)), dma((8,)), dma((8,)), dma((8,)), dma((8,)), dma((4,)), dma((4,)),
            dma((3,)), dma((3,)), dma((5,)), dma((3,)), dma((8,)), dma((8,)),
            dma, dma, dma((3,)), dma((3,)), dma((6,)), dma((6,)),
        ],
        compiler_params=pltpu.CompilerParams(collective_id=0, has_side_effects=True, vmem_limit_bytes=56 * 2**20),
    )(features, weight_a.reshape(3456, 256), weight_b.reshape(27, 256, 512), cotangent)
    return (gf, ga.transpose(0, 1, 2, 4, 3), gb)


def solution(mesh):
    placed = (P("tm", "space", None, None), P(), P(), P(None, "space", "tm", None))
    return jax.shard_map(
        shards,
        mesh=mesh,
        in_specs=placed,
        out_specs=(
            P("tm", "space", None, None),
            P(None, None, None, None, ("tm", "space")),
            P(None, None, None, ("tm", "space"), None),
        ),
        check_vma=False,
    )
```
